512 devices in a mesh: dp: 8 (over x, core), azim: 16 (over z), axial: 4 (over y).
Axes of the slice: x: 4, y: 4, z: 16, core: 2. Of those that a mesh axis runs over, the one named last changes fastest.
Arguments:
- field: bfloat16 [8, 32, 256, 8192], P('dp', None, 'azim', 'axial'), may hold values from -6 to 6
- cotangent: bfloat16 [8, 32, 256, 8192], P('dp', None, 'azim', 'axial'), may hold values from -0.119628906 to 0.119628906
- spectral_weight: bfloat16 [2, 16, 16, 16, 32, 32], P(None, 'azim', 'axial'), may hold values from -1 to 1
- point_weight: bfloat16 [32, 32], replicated, may hold values from -1 to 1
- bias: float32 [32], replicated, may hold values from -3 to 3
Outputs:
- weight_grad: float32 [2, 16, 16, 16, 32, 32], P(None, 'azim', 'axial')
The draws below stay inside these ranges and needn't reach their ends.
All inputs are finite; a program needn't handle non-finite values.
Results may differ from the reference program's by a relative error of at most 0.0003.
Values sent between devices are 32-bit elements; how exact they have to be, the bound alone decides.
No kernel may reach another device: no remote copies, remote signals or barrier semaphores. Data moves between devices by JAX's collectives and lax.ppermute only.
A program may use at most 128 MiB of HBM per device.

```python
import math
import jax
import jax.numpy as jnp
from jax import lax

C = 32
NA = 256
NL = 128
NR = 64
K = 16
BATCH = 8


def shard_levels(stream_key, dims, split, least, top_value):
    loudness = 1.0
    for dim, parts in split:
        heights = jax.random.uniform(jax.random.fold_in(jax.random.fold_in(stream_key, 6), dim), (parts,), jnp.float32, least / len(split), top_value / len(split))
        loudness = loudness * jnp.repeat(jnp.exp(heights), dims[dim] // parts).reshape((-1,) + (1,) * (len(dims) - 1 - dim))
    return loudness


def bell_draw(key, shape, deviation, bound, split=(), kind=jnp.bfloat16):
    gain = shard_levels(key, shape, split, -0.22, 0.18) if split else 1.0
    drawn = jax.random.normal(key, shape, jnp.float32) * deviation * gain
    return jnp.minimum(jnp.maximum(drawn, -bound), bound).astype(kind)


def setup_inputs(seed: int = 0) -> dict:
    key_of = jax.random.split(jax.random.key(seed), 6)
    return {
        "field": bell_draw(key_of[0], (BATCH, C, NA, NL * NR), 1.0, 6.0, ((0, 8), (2, 16), (3, 4))),
        "cotangent": bell_draw(key_of[1], (BATCH, C, NA, NL * NR), 0.02, 0.119628906, ((0, 8), (2, 16), (3, 4))),
        "spectral_weight": bell_draw(key_of[2], (2, K, K, K, C, C), C ** -0.5, 1.0, ((1, 16), (2, 4))),
        "point_weight": bell_draw(key_of[3], (C, C), C ** -0.5, 1.0),
        "bias": bell_draw(key_of[4], (C,), 0.5, 3.0, (), jnp.float32),
    }


HIGH = lax.Precision.HIGHEST

def phase_table(positions, modes, length):
    turns = positions[:, None] * modes[None, :] % length
    angle = turns.astype(jnp.float32) * (2.0 * math.pi / length)
    return (jnp.cos(angle), jnp.sin(angle))

def all_tables():
    modes = jnp.arange(K, dtype=jnp.int32)
    radial = phase_table(jnp.arange(NR, dtype=jnp.int32), modes, NR)
    azimuth = phase_table(jnp.arange(NA, dtype=jnp.int32), modes, NA)
    axial = phase_table(jnp.arange(NL, dtype=jnp.int32), modes, NL)
    return (radial, azimuth, axial)

def analysis(field, tables):
    (cos_r, sin_r), (cos_a, sin_a), (cos_l, sin_l) = tables
    rad_re = jnp.einsum('cxyz,zr->crxy', field, cos_r, precision=HIGH)
    rad_im = -jnp.einsum('cxyz,zr->crxy', field, sin_r, precision=HIGH)
    az_re = jnp.einsum('crxy,xa->cray', rad_re, cos_a, precision=HIGH) + jnp.einsum('crxy,xa->cray', rad_im, sin_a, precision=HIGH)
    az_im = jnp.einsum('crxy,xa->cray', rad_im, cos_a, precision=HIGH) - jnp.einsum('crxy,xa->cray', rad_re, sin_a, precision=HIGH)
    full_re = jnp.einsum('cray,yl->cral', az_re, cos_l, precision=HIGH) + jnp.einsum('cray,yl->cral', az_im, sin_l, precision=HIGH)
    full_im = jnp.einsum('cray,yl->cral', az_im, cos_l, precision=HIGH) - jnp.einsum('cray,yl->cral', az_re, sin_l, precision=HIGH)
    return (full_re, full_im)

def synthesis(spec_re, spec_im, tables):
    (cos_r, sin_r), (cos_a, sin_a), (cos_l, sin_l) = tables
    ax_re = jnp.einsum('oral,yl->oray', spec_re, cos_l, precision=HIGH) - jnp.einsum('oral,yl->oray', spec_im, sin_l, precision=HIGH)
    ax_im = jnp.einsum('oral,yl->oray', spec_re, sin_l, precision=HIGH) + jnp.einsum('oral,yl->oray', spec_im, cos_l, precision=HIGH)
    az_re = jnp.einsum('oray,xa->orxy', ax_re, cos_a, precision=HIGH) - jnp.einsum('oray,xa->orxy', ax_im, sin_a, precision=HIGH)
    az_im = jnp.einsum('oray,xa->orxy', ax_re, sin_a, precision=HIGH) + jnp.einsum('oray,xa->orxy', ax_im, cos_a, precision=HIGH)
    return jnp.einsum('orxy,zr->oxyz', az_re, cos_r, precision=HIGH) - jnp.einsum('orxy,zr->oxyz', az_im, sin_r, precision=HIGH)

def reference(field, cotangent, spectral_weight, point_weight, bias):
    tables = all_tables()
    field = field.reshape(BATCH, C, NA, NL, NR)
    cotangent = cotangent.reshape(BATCH, C, NA, NL, NR)
    weight_re = spectral_weight[0].astype(jnp.float32)
    weight_im = spectral_weight[1].astype(jnp.float32)
    point = point_weight.astype(jnp.float32)
    forward_scale = 1.0 / math.sqrt(NA * NL * NR)
    mode_scale = 1.0 / (K * math.sqrt(K))

    def one_sample(total, pair):
        sample, grad_out = pair
        values = sample.astype(jnp.float32)
        spec_re, spec_im = analysis(values, tables)
        spec_re = spec_re * forward_scale
        spec_im = spec_im * forward_scale
        mixed_re = jnp.einsum('cral,ralco->oral', spec_re, weight_re, precision=HIGH) - jnp.einsum('cral,ralco->oral', spec_im, weight_im, precision=HIGH)
        mixed_im = jnp.einsum('cral,ralco->oral', spec_re, weight_im, precision=HIGH) + jnp.einsum('cral,ralco->oral', spec_im, weight_re, precision=HIGH)
        back = synthesis(mixed_re, mixed_im, tables) * mode_scale
        pre = back + jnp.einsum('oc,cxyz->oxyz', point, values, precision=HIGH) + bias[:, None, None, None]
        _, pull = jax.vjp(jax.nn.gelu, pre)
        delta = pull(grad_out.astype(jnp.float32))[0]
        dmix_re, dmix_im = analysis(delta, tables)
        dmix_re = dmix_re * mode_scale
        dmix_im = dmix_im * mode_scale
        grad_re = jnp.einsum('cral,oral->ralco', spec_re, dmix_re, precision=HIGH) + jnp.einsum('cral,oral->ralco', spec_im, dmix_im, precision=HIGH)
        grad_im = jnp.einsum('cral,oral->ralco', spec_re, dmix_im, precision=HIGH) - jnp.einsum('cral,oral->ralco', spec_im, dmix_re, precision=HIGH)
        return (total + jnp.stack([grad_re, grad_im]), None)
    start = jnp.zeros((2, K, K, K, C, C), jnp.float32)
    total, _ = lax.scan(one_sample, start, (field, cotangent))
    return total
```

```python
import math

import jax
import jax.numpy as jnp
import ml_dtypes
import numpy as np
from jax import lax
from jax.experimental import pallas as pl
from jax.experimental.pallas import tpu as pltpu
from jax.sharding import PartitionSpec as P

NR = 64
BF = jnp.bfloat16
F32 = jnp.float32
LANE_STEPS = 4
VMEM = 60 * 1024 * 1024


def split_table(values):
    high = values.astype(ml_dtypes.bfloat16)
    low = (values - high.astype(np.float64)).astype(ml_dtypes.bfloat16)
    return high, low


def split(values):
    high = values.astype(BF)
    return high, (values - high.astype(F32)).astype(BF)


def split3(values):
    high = values.astype(BF)
    rest = values - high.astype(F32)
    mid = rest.astype(BF)
    return high, mid, (rest - mid.astype(F32)).astype(BF)


def dot(a, b):
    return lax.dot_general(a, b, (((1,), (0,)), ((), ())), preferred_element_type=F32)


def dot_nt(a, b):
    return lax.dot_general(a, b, (((1,), (1,)), ((), ())), preferred_element_type=F32)


def dot_tn(a, b):
    return lax.dot_general(a, b, (((0,), (0,)), ((), ())), preferred_element_type=F32)


class Tables:
    def __init__(self, modes, chans, cells_a, cells_l, cells_r, n_azim, n_axial):
        total_a, total_l = cells_a * n_azim, cells_l * n_axial
        k = np.arange(modes, dtype=np.float64)
        radial = np.outer(k, np.arange(cells_r)) / cells_r
        axial = np.outer(k, np.arange(cells_l)) / total_l
        angle = 2.0 * np.pi * (radial[:, None, None, :] + axial[None, :, :, None])
        angle = angle.reshape(modes * modes, cells_l * cells_r)
        self.cells = split_table(np.concatenate([np.cos(angle), -np.sin(angle)], 0))
        angle = 2.0 * np.pi * np.outer(np.arange(cells_a), k) / total_a
        same = np.eye(chans)

        def spread(table):
            whole = table[None, :, :, None] * same[:, None, None, :]
            return whole.reshape(chans * cells_a, modes * chans)

        self.turn = split_table(spread(np.cos(angle))) + split_table(spread(np.sin(angle)))
        quarter = 0.5 * np.pi * (np.outer(np.arange(n_axial), k) % 4 if n_axial == 4 else np.outer(np.arange(n_axial), k) * (4 / n_axial))
        self.axial_cos = np.repeat(np.cos(quarter).round(15)[:, :, None], 128, 2).astype(np.float32)
        self.axial_sin = np.repeat(np.sin(quarter).round(15)[:, :, None], 128, 2).astype(np.float32)
        loc_a = modes // n_axial
        turns = np.outer(np.arange(n_azim), k) / n_azim
        turns = turns.reshape(n_azim, n_axial, loc_a).transpose(1, 0, 2)
        turns = np.repeat(turns, chans, 2) * (2.0 * np.pi)
        self.azim_cos = np.cos(turns).astype(np.float32)
        self.azim_sin = np.sin(turns).astype(np.float32)


def azimuth_analysis(values, turn, out_ref):
    cos_h, cos_l, sin_h, sin_l = (r[...] for r in turn)
    high, low = split(values)
    by_cos = dot(high, cos_h) + dot(low, cos_h) + dot(high, cos_l)
    by_sin = dot(high, sin_h) + dot(low, sin_h) + dot(high, sin_l)
    half = values.shape[0] // 2
    real = by_cos[:half] + by_sin[half:]
    imag = by_cos[half:] - by_sin[:half]
    groups, n_kr, rows, lanes = out_ref.shape
    n_kl = rows // 2
    for g in range(groups):
        at = slice(g * lanes, (g + 1) * lanes)
        out_ref[g, :, :n_kl, :] = real[:, at].reshape(n_kr, n_kl, lanes)
        out_ref[g, :, n_kl:, :] = imag[:, at].reshape(n_kr, n_kl, lanes)


def analysis_kernel(field, cells_h, cells_l, cos_h, cos_l, sin_h, sin_l, out, total):
    step = pl.program_id(0)
    x = field[...]
    part = dot_nt(cells_h[...], x) + dot_nt(cells_l[...], x)

    @pl.when(step == 0)
    def _():
        total[...] = part

    @pl.when(step > 0)
    def _():
        total[...] += part

    @pl.when(step == pl.num_programs(0) - 1)
    def _():
        azimuth_analysis(total[...], (cos_h, cos_l, sin_h, sin_l), out)


def layer_kernel(
    mixed, field, cot, mix, bias, cells_h, cells_l, cos_h, cos_l, sin_h, sin_l, out, synth_h, synth_l, total
):
    step = pl.program_id(0)

    @pl.when(step == 0)
    def _():
        groups, n_kr, rows, lanes = mixed.shape
        n_kl = rows // 2

        def gather(at):
            parts = [mixed[g, :, at, :].reshape(n_kr * n_kl, lanes) for g in range(groups)]
            return jnp.concatenate(parts, 1)

        re_h, re_l = split(gather(slice(0, n_kl)))
        im_h, im_l = split(gather(slice(n_kl, rows)))
        c_h, c_l, s_h, s_l = cos_h[...], cos_l[...], sin_h[...], sin_l[...]

        def times(t_h, t_l, v_h, v_l):
            return dot_nt(t_h, v_h) + dot_nt(t_h, v_l) + dot_nt(t_l, v_h)

        real = times(c_h, c_l, re_h, re_l) - times(s_h, s_l, im_h, im_l)
        imag = times(s_h, s_l, re_h, re_l) + times(c_h, c_l, im_h, im_l)
        half = real.shape[1]
        high, low = split(real)
        synth_h[:, :half] = high
        synth_l[:, :half] = low
        high, low = split(imag)
        synth_h[:, half:] = high
        synth_l[:, half:] = low

    t_h = cells_h[...]
    t_l = cells_l[...]
    s_h = synth_h[...]
    pre = dot(s_h, t_h) + dot(synth_l[...], t_h) + dot(s_h, t_l)
    pre = pre + dot(mix[...], field[...]) + bias[...]
    slope = math.sqrt(2.0 / math.pi)
    square = pre * pre
    t = jnp.tanh(pre * (slope + (slope * 0.044715) * square))
    inner = slope + (3.0 * slope * 0.044715) * square
    grad = 0.5 * (1.0 + t) + (0.5 * pre) * (1.0 - t * t) * inner
    d_h, d_l = split(cot[...].astype(F32) * grad)
    part = dot_nt(t_h, d_h) + dot_nt(t_h, d_l) + dot_nt(t_l, d_h)

    @pl.when(step == 0)
    def _():
        total[...] = part

    @pl.when(step > 0)
    def _():
        total[...] += part

    @pl.when(step == pl.num_programs(0) - 1)
    def _():
        azimuth_analysis(total[...], (cos_h, cos_l, sin_h, sin_l), out)


def axial_sum_kernel(parts, cos, sin, out):
    groups, _, rows, _ = parts.shape
    n_kl = rows // 2
    real = parts[0, :, :n_kl, :]
    imag = parts[0, :, n_kl:, :]
    for g in range(1, groups):
        re, im = parts[g, :, :n_kl, :], parts[g, :, n_kl:, :]
        c, s = cos[g][None], sin[g][None]
        real += re * c + im * s
        imag += im * c - re * s
    out[:, :n_kl, :] = real
    out[:, n_kl:, :] = imag


def axial_spread_kernel(values, cos, sin, out):
    groups, _, rows, _ = out.shape
    n_kl = rows // 2
    re, im = values[:, :n_kl, :], values[:, n_kl:, :]
    for g in range(groups):
        c, s = cos[g][None], sin[g][None]
        out[g, :, :n_kl, :] = re * c - im * s
        out[g, :, n_kl:, :] = im * c + re * s


def azim_sum(parts, cos, sin, n_kl, scale):
    real = imag = None
    for z in range(parts.shape[0]):
        re, im = parts[z, :n_kl, :], parts[z, n_kl:, :]
        c, s = cos[z : z + 1, :], sin[z : z + 1, :]
        a, b = re * c + im * s, im * c - re * s
        real, imag = (a, b) if z == 0 else (real + a, imag + b)
    return real * scale, imag * scale


def mix_kernel(scale, out_scale, parts, weight, cos, sin, spec, out):
    n_azim, rows, lanes = parts.shape
    n_kl = rows // 2
    y = lax.axis_index("axial")
    c, s = cos[y], sin[y]
    real, imag = azim_sum(parts, c, s, n_kl, scale)
    spec[:n_kl, :] = real
    spec[n_kl:, :] = imag
    stack = jnp.concatenate([*split3(real), *split3(imag)], 0)
    row = lax.broadcasted_iota(jnp.int32, (stack.shape[0], 2 * lanes), 0) % n_kl
    got = jnp.zeros((stack.shape[0], 2 * lanes), F32)
    for kl in range(n_kl):
        got = jnp.where(row == kl, dot(stack, weight[kl]), got)
    by_re = got[:n_kl] + got[n_kl : 2 * n_kl] + got[2 * n_kl : 3 * n_kl]
    by_im = got[3 * n_kl : 4 * n_kl] + got[4 * n_kl : 5 * n_kl] + got[5 * n_kl :]
    re = (by_re[:, :lanes] - by_im[:, lanes:]) * out_scale
    im = (by_re[:, lanes:] + by_im[:, :lanes]) * out_scale
    for z in range(n_azim):
        cz, sz = c[z : z + 1, :], s[z : z + 1, :]
        out[z, :n_kl, :] = re * cz - im * sz
        out[z, n_kl:, :] = im * cz + re * sz


def join_kernel(scale, parts, spec, cos, sin, out):
    rows = parts.shape[1]
    n_kl = rows // 2
    y = lax.axis_index("axial")
    real, imag = azim_sum(parts, cos[y], sin[y], n_kl, scale)
    for d in range(out.shape[0]):
        out[d, :rows, :] = spec[...]
        out[d, rows : rows + n_kl, :] = real
        out[d, rows + n_kl :, :] = imag


def grad_kernel(pairs, out):
    _, n_ka, n_kl, chans, _ = out.shape
    lanes = pairs.shape[2]
    for kl in range(n_kl):
        s_re, s_im, d_re, d_im = (pairs[:, i * n_kl + kl, :] for i in range(4))
        s_h, s_l = split(jnp.concatenate([s_re, s_im], 0))
        a = jnp.concatenate([d_re, d_im], 0)
        b = jnp.concatenate([d_im, -d_re], 0)
        d_h, d_l = split(jnp.concatenate([a, b], 1))
        left = jnp.concatenate([s_h, s_l, s_h], 0)
        right = jnp.concatenate([d_h, d_h, d_l], 0)
        whole = dot_tn(left, right)
        for ka in range(n_ka):
            at = slice(ka * chans, (ka + 1) * chans)
            for q in range(2):
                lo = q * lanes + ka * chans
                out[q, ka, kl] = whole[at, lo : lo + chans]


def call(kernel, out_shape, *args, **more):
    return pl.pallas_call(
        kernel,
        out_shape=out_shape,
        compiler_params=pltpu.CompilerParams(vmem_limit_bytes=VMEM),
        **more,
    )(*args)


def per_device(field, cotangent, spectral_weight, point_weight, bias):
    samples, chans, cells_a, merged = field.shape
    cells_r = NR
    cells_l = merged // cells_r
    n_azim = lax.axis_size("azim")
    n_axial = lax.axis_size("axial")
    n_dp = lax.axis_size("dp")
    _, _, loc_a, modes, _, _ = spectral_weight.shape
    tables = Tables(modes, chans, cells_a, cells_l, cells_r, n_azim, n_axial)
    total_cells = cells_a * n_azim * cells_l * n_axial * cells_r
    forward_scale = 1.0 / math.sqrt(total_cells)
    mode_scale = 1.0 / (modes * math.sqrt(modes))
    rows_x = chans * cells_a
    rows_k = 2 * modes * modes
    lanes = loc_a * chans
    block = (2 * modes, lanes)
    whole = jax.ShapeDtypeStruct((n_axial, modes, *block), F32)
    ring = jax.ShapeDtypeStruct((n_azim, *block), F32)
    cells = [jnp.asarray(t) for t in tables.cells]
    turn = [jnp.asarray(t) for t in tables.turn]
    axial_phase = (jnp.asarray(tables.axial_cos), jnp.asarray(tables.axial_sin))
    azim_phase = (jnp.asarray(tables.azim_cos), jnp.asarray(tables.azim_sin))

    x = field.reshape(rows_x, merged)
    cot = cotangent.reshape(rows_x, merged)
    weight = spectral_weight[:, 0].transpose(2, 1, 3, 0, 4)
    weight = weight[:, :, :, :, None, :] * jnp.eye(loc_a, dtype=BF)[None, :, None, None, :, None]
    weight = weight.reshape(modes, lanes, 2 * lanes)
    mix = point_weight[:, None, :, None] * jnp.eye(cells_a, dtype=BF)[None, :, None, :]
    mix = mix.reshape(rows_x, rows_x)
    bias_rows = jnp.repeat(bias, cells_a)[:, None]

    step = merged // LANE_STEPS
    lane_spec = pl.BlockSpec((rows_x, step), lambda i: (0, i))
    cell_spec = pl.BlockSpec((rows_k, step), lambda i: (0, i))

    def fixed(array):
        return pl.BlockSpec(array.shape, lambda i: (0,) * array.ndim)

    total = pltpu.VMEM((rows_k, rows_x), F32)

    def reduce(values):
        values = lax.all_to_all(values, "axial", 0, 0, tiled=True)
        values = call(axial_sum_kernel, ring, values, *axial_phase)
        return lax.all_to_all(values, "azim", 0, 0, tiled=True)

    first = call(
        analysis_kernel,
        whole,
        x,
        *cells,
        *turn,
        grid=(LANE_STEPS,),
        in_specs=[lane_spec, cell_spec, cell_spec, *map(fixed, turn)],
        out_specs=fixed(whole),
        scratch_shapes=[total],
    )
    parts = reduce(first)

    def mix_body(*refs):
        mix_kernel(forward_scale, mode_scale, *refs)

    spec, mixed = call(
        mix_body, (jax.ShapeDtypeStruct(block, F32), ring), parts, weight, *azim_phase
    )
    mixed = lax.all_to_all(mixed, "azim", 0, 0, tiled=True)
    mixed = call(axial_spread_kernel, whole, mixed, *axial_phase)
    mixed = lax.all_to_all(mixed, "axial", 0, 0, tiled=True)
    synth = pltpu.VMEM((rows_x, rows_k), BF)
    second = call(
        layer_kernel,
        whole,
        mixed,
        x,
        cot,
        mix,
        bias_rows,
        *cells,
        *turn,
        grid=(LANE_STEPS,),
        in_specs=[fixed(whole), lane_spec, lane_spec, fixed(mix), fixed(bias_rows), cell_spec, cell_spec, *map(fixed, turn)],
        out_specs=fixed(whole),
        scratch_shapes=[synth, synth, total],
    )
    parts = reduce(second)

    def join_body(*refs):
        join_kernel(mode_scale, *refs)

    pairs = call(
        join_body, jax.ShapeDtypeStruct((n_dp, 2 * block[0], lanes), F32), parts, spec, *azim_phase
    )
    pairs = lax.all_to_all(pairs, "dp", 0, 0, tiled=True)
    grad = call(grad_kernel, jax.ShapeDtypeStruct((2, loc_a, modes, chans, chans), F32), pairs)
    return grad[:, None]


def solution(mesh):
    in_specs = (
        P("dp", None, "azim", "axial"),
        P("dp", None, "azim", "axial"),
        P(None, "azim", "axial", None, None, None),
        P(),
        P(),
    )
    out_specs = P(None, "azim", "axial", None, None, None)
    return jax.shard_map(
        per_device, mesh=mesh, in_specs=in_specs, out_specs=out_specs, check_vma=False
    )
```

```python
import math

import jax
import jax.numpy as jnp
import ml_dtypes
import numpy as np
from jax import lax
from jax.experimental import pallas as pl
from jax.experimental.pallas import tpu as pltpu
from jax.sharding import Mesh
from jax.sharding import PartitionSpec as P

NR = 64
NEAR = 2
BF = jnp.bfloat16
F32 = jnp.float32
FIRST_CHUNKS = 4
LAYER_CHUNKS = 4
LOCAL_CHUNKS = 2
VMEM = 40 * 1024 * 1024


def split_table(values):
    high = values.astype(ml_dtypes.bfloat16)
    low = (values - high.astype(np.float64)).astype(ml_dtypes.bfloat16)
    return high, low


def split(values):
    high = values.astype(BF)
    return high, (values - high.astype(F32)).astype(BF)


def split3(values):
    high = values.astype(BF)
    rest = values - high.astype(F32)
    mid = rest.astype(BF)
    return high, mid, (rest - mid.astype(F32)).astype(BF)


def dot(a, b):
    return lax.dot_general(a, b, (((1,), (0,)), ((), ())), preferred_element_type=F32)


def dot_nt(a, b):
    return lax.dot_general(a, b, (((1,), (1,)), ((), ())), preferred_element_type=F32)


def dot_tn(a, b):
    return lax.dot_general(a, b, (((0,), (0,)), ((), ())), preferred_element_type=F32)


class Tables:
    def __init__(self, modes, chans, cells_a, cells_l, cells_r, n_azim, n_axial):
        total_a, total_l = cells_a * n_azim, cells_l * n_axial
        k = np.arange(modes)
        radial = np.outer(k, np.arange(cells_r)) % cells_r / cells_r
        radial = radial.reshape(modes // NEAR, NEAR, cells_r).transpose(1, 0, 2).reshape(modes, cells_r)
        axial = np.outer(k, np.arange(cells_l)) % total_l / total_l
        angle = 2.0 * np.pi * (radial[:, None, None, :] + axial[None, :, :, None])
        angle = angle.reshape(modes * modes, cells_l * cells_r)
        self.cells = split_table(np.concatenate([np.cos(angle), -np.sin(angle)], 0))
        half = chans // 2
        angle = 2.0 * np.pi * np.outer(np.arange(cells_a), k) / total_a
        same = np.eye(half)

        def spread(table):
            whole = table[None, :, :, None] * same[:, None, None, :]
            return whole.reshape(half * cells_a, modes * half)

        self.turn = np.stack(split_table(spread(np.cos(angle))) + split_table(spread(np.sin(angle))))
        loc_a = modes // n_axial
        axial = (np.outer(np.arange(n_axial) * cells_l, k) % total_l / total_l).reshape(1, n_axial, modes, 1)
        azim = (np.outer(np.arange(n_azim) * cells_a, k) % total_a / total_a).reshape(n_azim, n_axial, 1, loc_a, 1)
        azim = np.broadcast_to(azim, (n_azim, n_axial, 2, loc_a, half)).reshape(n_azim, 1, 1, modes * chans)
        angle = 2.0 * np.pi * (axial + azim)
        self.place = np.stack([np.cos(angle), np.sin(angle)], 2).astype(np.float32)


def azimuth_analysis(values, turn, place, out_ref):
    cos_h, cos_l, sin_h, sin_l = (turn[i] for i in range(4))
    rows, cols = values.shape[0] // 2, values.shape[1] // 2
    near, groups, far, block, lanes = out_ref.shape
    n_kl = block // 2
    reals, imags = [], []
    for h in range(2):
        high, low = split(values[:, h * cols : (h + 1) * cols])
        by_cos = dot(high, cos_h) + dot(low, cos_h) + dot(high, cos_l)
        by_sin = dot(high, sin_h) + dot(low, sin_h) + dot(high, sin_l)
        reals.append(by_cos[:rows] + by_sin[rows:])
        imags.append(by_cos[rows:] - by_sin[:rows])
    for g in range(groups):
        at = slice(g * lanes // 2, (g + 1) * lanes // 2)
        re = jnp.concatenate([r[:, at] for r in reals], 1).reshape(near, far, n_kl, lanes)
        im = jnp.concatenate([i[:, at] for i in imags], 1).reshape(near, far, n_kl, lanes)
        to = slice(g * lanes, (g + 1) * lanes)
        c, s = place[0, :, to], place[1, :, to]
        out_ref[:, g, :, :n_kl, :] = re * c + im * s
        out_ref[:, g, :, n_kl:, :] = im * c - re * s


def azimuth_synthesis(mixed, turn, place, synth_h, synth_l):
    near, groups, far, block, lanes = mixed.shape
    n_kl = block // 2
    rows = near * far * n_kl
    reals, imags = [], []
    for g in range(groups):
        re, im = mixed[:, g, :, :n_kl, :], mixed[:, g, :, n_kl:, :]
        to = slice(g * lanes, (g + 1) * lanes)
        c, s = place[0, :, to], place[1, :, to]
        reals.append((re * c - im * s).reshape(rows, lanes))
        imags.append((im * c + re * s).reshape(rows, lanes))
    cos_h, cos_l, sin_h, sin_l = (turn[i] for i in range(4))

    def times(t_h, t_l, v):
        return dot_nt(t_h, v[0]) + dot_nt(t_h, v[1]) + dot_nt(t_l, v[0])

    half = synth_h.shape[0] // 2
    for h in range(2):
        at = slice(h * lanes // 2, (h + 1) * lanes // 2)
        re = split(jnp.concatenate([r[:, at] for r in reals], 1))
        im = split(jnp.concatenate([i[:, at] for i in imags], 1))
        real = times(cos_h, cos_l, re) - times(sin_h, sin_l, im)
        imag = times(sin_h, sin_l, re) + times(cos_h, cos_l, im)
        to = slice(h * half, (h + 1) * half)
        for q, part in enumerate((real, imag)):
            high, low = split(part)
            synth_h[to, q * rows : (q + 1) * rows] = high
            synth_l[to, q * rows : (q + 1) * rows] = low


def start_chunks(pairs, sems, chunks):
    step = pairs[0][0].shape[1] // chunks
    copies = []
    for i in range(chunks):
        at = pl.ds(i * step, step)
        copies.append([pltpu.make_async_copy(a.at[:, at], b.at[:, at], sems.at[i, j]) for j, (a, b) in enumerate(pairs)])
        for copy in copies[-1]:
            copy.start()
    return step, copies


def analysis_kernel(field, cells_h, cells_l, turn, place, out, turn_here, place_here, x, t_h, t_l, total, sems, more_sems):
    step, copies = start_chunks(((field, x), (cells_h, t_h), (cells_l, t_l)), sems, FIRST_CHUNKS)
    y = lax.axis_index("axial")
    z = lax.axis_index("zh") * NEAR + lax.axis_index("zl")
    more = [
        pltpu.make_async_copy(turn, turn_here, more_sems.at[0]),
        pltpu.make_async_copy(place.at[z, y], place_here, more_sems.at[1]),
    ]
    for copy in more:
        copy.start()
    for i in range(FIRST_CHUNKS):
        for copy in copies[i]:
            copy.wait()
        at = slice(i * step, (i + 1) * step)
        values = x[:, at]
        part = dot_nt(t_h[:, at], values) + dot_nt(t_l[:, at], values)
        total[...] = part if i == 0 else total[...] + part
    for copy in more:
        copy.wait()
    azimuth_analysis(total[...], turn_here, place_here, out)


def layer_kernel(
    mixed, turn, place, local_far, cot_far, cells_h, cells_l, out,
    synth_h, synth_l, delta_h, delta_l, local, cot, all_h, all_l, sems,
):
    pairs = ((cells_h, all_h), (cells_l, all_l), (local_far, local), (cot_far, cot))
    step, copies = start_chunks(pairs, sems, LAYER_CHUNKS)
    azimuth_synthesis(mixed, turn, place, synth_h, synth_l)
    s_h, s_l = synth_h[...], synth_l[...]
    slope = math.sqrt(2.0 / math.pi)
    for i in range(LAYER_CHUNKS):
        for copy in copies[i]:
            copy.wait()
        at = slice(i * step, (i + 1) * step)
        t_h = all_h[:, at]
        pre = dot(s_h, t_h) + dot(s_l, t_h) + dot(s_h, all_l[:, at]) + local[:, at]
        square = pre * pre
        t = jnp.tanh(pre * (slope + (slope * 0.044715) * square))
        inner = slope + (3.0 * slope * 0.044715) * square
        grad = 0.5 * (1.0 + t) + (0.5 * pre) * (1.0 - t * t) * inner
        delta_h[:, at], delta_l[:, at] = split(cot[:, at].astype(F32) * grad)
    t_h, d_h = all_h[...], delta_h[...]
    total = dot_nt(t_h, d_h) + dot_nt(t_h, delta_l[...]) + dot_nt(all_l[...], d_h)
    azimuth_analysis(total, turn, place, out)


def prepare_kernel(
    weight_far, point_far, bias_far, field, out_weight, local_far, weight, point, bias, x, local, sems, chunk_sems, out_sems
):
    small = ((point_far, point), (bias_far, bias), (weight_far, weight))
    copies = [pltpu.make_async_copy(a, b, sems.at[i]) for i, (a, b) in enumerate(small)]
    for copy in copies:
        copy.start()
    step, chunks = start_chunks(((field, x),), chunk_sems, LOCAL_CHUNKS)
    n_q, n_ka, n_kl, chans, _ = weight.shape
    rows = x.shape[0]
    cells = rows // chans

    def owner(shape, axis):
        i, c = lax.broadcasted_iota(jnp.int32, shape, axis), lax.broadcasted_iota(jnp.int32, shape, 1 - axis)
        return (i >= c * cells) & (i < (c + 1) * cells)

    left = owner((rows, chans), 0)
    right = jnp.where(owner((chans, rows), 1), 1.0, 0.0).astype(BF)
    i = lax.broadcasted_iota(jnp.int32, (rows, rows), 0)
    j = lax.broadcasted_iota(jnp.int32, (rows, rows), 1)
    copies[0].wait()
    copies[1].wait()
    wide = dot(dot(jnp.where(left, 1.0, 0.0).astype(BF), point[...]).astype(BF), right)
    mix = jnp.where(i % cells == j % cells, wide, 0.0).astype(BF)
    shift = jnp.sum(jnp.where(left, bias[...], 0.0), 1, keepdims=True)
    sends = []
    for i in range(LOCAL_CHUNKS):
        chunks[i][0].wait()
        at = slice(i * step, (i + 1) * step)
        local[:, at] = dot(mix, x[:, at]) + shift
        to = pl.ds(i * step, step)
        sends.append(pltpu.make_async_copy(local.at[:, to], local_far.at[:, to], out_sems.at[i]))
        sends[-1].start()
    half = chans // 2
    lanes = n_ka * chans
    o = lax.broadcasted_iota(jnp.int32, (chans, lanes), 0)
    lane = lax.broadcasted_iota(jnp.int32, (chans, lanes), 1)
    copies[2].wait()
    for ka in range(n_ka):
        to = jnp.where(o < half, o, o + (n_ka - 1) * half) + ka * half
        place = jnp.where(lane == to, 1.0, 0.0).astype(BF)
        for q in range(n_q):
            moved = dot(weight[q, ka].reshape(n_kl * chans, chans), place).astype(BF)
            moved = moved.reshape(n_kl, 2, half, lanes)
            for h in range(2):
                at = h * lanes // 2 + ka * half
                out_weight[:, at : at + half, q * lanes : (q + 1) * lanes] = moved[:, h]
    for copy in sends:
        copy.wait()


def mix_kernel(scale, out_scale, parts, weight, spec, out):
    far, rows, lanes = parts.shape
    n_kl = rows // 2
    total = parts[0]
    for z in range(1, far):
        total = total + parts[z]
    total = total * scale
    spec[...] = total
    stack = jnp.concatenate([*split3(total[:n_kl]), *split3(total[n_kl:])], 0)
    row = lax.broadcasted_iota(jnp.int32, (stack.shape[0], 2 * lanes), 0) % n_kl
    got = jnp.zeros((stack.shape[0], 2 * lanes), F32)
    for kl in range(n_kl):
        got = jnp.where(row == kl, dot(stack, weight[kl]), got)
    by_re = got[:n_kl] + got[n_kl : 2 * n_kl] + got[2 * n_kl : 3 * n_kl]
    by_im = got[3 * n_kl : 4 * n_kl] + got[4 * n_kl : 5 * n_kl] + got[5 * n_kl :]
    re = (by_re[:, :lanes] - by_im[:, lanes:]) * out_scale
    im = (by_re[:, lanes:] + by_im[:, :lanes]) * out_scale
    for z in range(far):
        out[z, :n_kl, :] = re
        out[z, n_kl:, :] = im


def join_kernel(scale, parts, spec, out):
    far, rows, _ = parts.shape
    total = parts[0]
    for z in range(1, far):
        total = total + parts[z]
    total = total * scale
    for d in range(out.shape[0]):
        out[d, :rows, :] = spec[...]
        out[d, rows:, :] = total


def grad_kernel(pairs, out):
    _, n_ka, n_kl, chans, _ = out.shape
    half = chans // 2
    lanes = pairs.shape[2]
    for kl in range(n_kl):
        s_re, s_im, d_re, d_im = (pairs[:, i * n_kl + kl, :] for i in range(4))
        s_h, s_l = split(jnp.concatenate([s_re, s_im], 0))
        a = jnp.concatenate([d_re, d_im], 0)
        b = jnp.concatenate([d_im, -d_re], 0)
        d_h, d_l = split(jnp.concatenate([a, b], 1))
        left = jnp.concatenate([s_h, s_l, s_h], 0)
        right = jnp.concatenate([d_h, d_h, d_l], 0)
        whole = dot_tn(left, right)
        for q in range(2):
            for ka in range(n_ka):
                for h in range(2):
                    r = h * lanes // 2 + ka * half
                    for g in range(2):
                        c = q * lanes + g * lanes // 2 + ka * half
                        out[q, ka, kl, h * half : (h + 1) * half, g * half : (g + 1) * half] = whole[r : r + half, c : c + half]


def call(kernel, out_shape, *args, **more):
    return pl.pallas_call(
        kernel,
        out_shape=out_shape,
        compiler_params=pltpu.CompilerParams(vmem_limit_bytes=VMEM),
        **more,
    )(*args)


def shape(*dims, dtype=F32):
    return jax.ShapeDtypeStruct(dims, dtype)


def per_device(field, cotangent, spectral_weight, point_weight, bias):
    _, chans, cells_a, merged = field.shape
    cells_r = NR
    cells_l = merged // cells_r
    far, n_axial, n_dp = (lax.axis_size(name) for name in ("zh", "axial", "dp"))
    n_azim = far * NEAR
    _, _, loc_a, modes, _, _ = spectral_weight.shape
    tables = Tables(modes, chans, cells_a, cells_l, cells_r, n_azim, n_axial)
    total_cells = cells_a * n_azim * cells_l * n_axial * cells_r
    forward_scale = 1.0 / math.sqrt(total_cells)
    mode_scale = 1.0 / (modes * math.sqrt(modes))
    rows_x = chans * cells_a
    rows_k = 2 * modes * modes
    lanes = loc_a * chans
    block = (2 * modes, lanes)
    whole = (NEAR, n_axial, far, *block)
    cells = [jnp.asarray(t) for t in tables.cells]
    turn, place = jnp.asarray(tables.turn), jnp.asarray(tables.place)
    x = field.reshape(rows_x, merged)
    cot = cotangent.reshape(rows_x, merged)
    near_axes = ("zl", "axial")

    def exchange(values, axes):
        flat = values.reshape(-1, *block)
        return lax.all_to_all(flat, axes, 0, 0, tiled=True).reshape(values.shape)

    def reduce(values):
        return exchange(exchange(values, near_axes).sum((0, 1)), "zh")

    far_off = pl.BlockSpec(memory_space=pl.ANY)
    near_by = pl.BlockSpec(memory_space=pltpu.VMEM)

    def stay(array):
        return pltpu.with_memory_space_constraint(array, pltpu.HBM)

    field_shape = pltpu.VMEM((rows_x, merged), BF)
    local_shape = pltpu.VMEM((rows_x, merged), F32)
    cell_shape = pltpu.VMEM((rows_k, merged), BF)
    x, cot, turn, place = map(stay, (x, cot, turn, place))
    cells = [*map(stay, cells)]
    first, turn, place = call(
        analysis_kernel,
        (pltpu.VMEM(whole, F32), pltpu.VMEM(turn.shape, BF), pltpu.VMEM(place.shape[2:], F32)),
        x,
        *cells,
        turn,
        place,
        in_specs=[far_off] * 5,
        out_specs=[near_by] * 3,
        scratch_shapes=[
            field_shape,
            cell_shape,
            cell_shape,
            pltpu.VMEM((rows_k, rows_x), F32),
            pltpu.SemaphoreType.DMA((FIRST_CHUNKS, 3)),
            pltpu.SemaphoreType.DMA((2,)),
        ],
    )
    weight_shape = spectral_weight[:, 0].shape
    weight, local = call(
        prepare_kernel,
        (pltpu.VMEM((modes, lanes, 2 * lanes), BF), pltpu.HBM((rows_x, merged), F32)),
        *map(stay, (spectral_weight[:, 0], point_weight, bias[None], x)),
        in_specs=[far_off] * 4,
        out_specs=[near_by, far_off],
        scratch_shapes=[
            pltpu.VMEM(weight_shape, BF),
            pltpu.VMEM(point_weight.shape, BF),
            pltpu.VMEM((1, chans), F32),
            field_shape,
            local_shape,
            pltpu.SemaphoreType.DMA((3,)),
            pltpu.SemaphoreType.DMA((LOCAL_CHUNKS, 1)),
            pltpu.SemaphoreType.DMA((LOCAL_CHUNKS,)),
        ],
    )
    parts = reduce(first)

    def mix_body(*refs):
        mix_kernel(forward_scale, mode_scale, *refs)

    spec, mixed = call(mix_body, (shape(*block), shape(far, *block)), parts, weight)
    mixed = exchange(mixed, "zh")
    mixed = exchange(jnp.broadcast_to(mixed, whole), near_axes)
    synth = pltpu.VMEM((rows_x, rows_k), BF)
    delta = pltpu.VMEM((rows_x, merged), BF)
    second = call(
        layer_kernel,
        pltpu.VMEM(whole, F32),
        mixed,
        turn,
        place,
        stay(local),
        cot,
        *cells,
        in_specs=[near_by] * 3 + [far_off] * 4,
        out_specs=near_by,
        scratch_shapes=[
            synth,
            synth,
            delta,
            delta,
            local_shape,
            field_shape,
            cell_shape,
            cell_shape,
            pltpu.SemaphoreType.DMA((LAYER_CHUNKS, 4)),
        ],
    )
    parts = reduce(second)

    def join_body(*refs):
        join_kernel(mode_scale, *refs)

    pairs = call(join_body, shape(n_dp, 2 * block[0], lanes), parts, spec)
    pairs = lax.all_to_all(pairs, "dp", 0, 0, tiled=True)
    grad = call(grad_kernel, shape(2, loc_a, modes, chans, chans), pairs)
    return grad[:, None]


def solution(mesh):
    n_dp, n_azim, n_axial = (mesh.shape[name] for name in ("dp", "azim", "axial"))
    fine = Mesh(mesh.devices.reshape(n_dp, n_azim // NEAR, NEAR, n_axial), ("dp", "zh", "zl", "axial"))
    azim = ("zh", "zl")
    in_specs = (
        P("dp", None, azim, "axial"),
        P("dp", None, azim, "axial"),
        P(None, azim, "axial", None, None, None),
        P(),
        P(),
    )
    out_specs = P(None, azim, "axial", None, None, None)
    return jax.shard_map(
        per_device, mesh=fine, in_specs=in_specs, out_specs=out_specs, check_vma=False
    )
```

```python
import math

import jax
import jax.numpy as jnp
import ml_dtypes
import numpy as np
from jax import lax
from jax.experimental import pallas as pl
from jax.experimental.pallas import tpu as pltpu
from jax.sharding import Mesh
from jax.sharding import PartitionSpec as P

NR = 64
NEAR = 2
BF = jnp.bfloat16
F32 = jnp.float32
GROUPS = 4
LOCAL_CHUNKS = 2
VMEM = 40 * 1024 * 1024


def split_table(values):
    high = values.astype(ml_dtypes.bfloat16)
    low = (values - high.astype(np.float64)).astype(ml_dtypes.bfloat16)
    return high, low


def split(values):
    high = values.astype(BF)
    return high, (values - high.astype(F32)).astype(BF)


def split3(values):
    high = values.astype(BF)
    rest = values - high.astype(F32)
    mid = rest.astype(BF)
    return high, mid, (rest - mid.astype(F32)).astype(BF)


def dot(a, b):
    return lax.dot_general(a, b, (((1,), (0,)), ((), ())), preferred_element_type=F32)


def dot_nt(a, b):
    return lax.dot_general(a, b, (((1,), (1,)), ((), ())), preferred_element_type=F32)


def dot_tn(a, b):
    return lax.dot_general(a, b, (((0,), (0,)), ((), ())), preferred_element_type=F32)


class Tables:
    def __init__(self, modes, chans, cells_a, cells_l, cells_r, n_azim, n_axial):
        total_a, total_l = cells_a * n_azim, cells_l * n_axial
        k = np.arange(modes)
        radial = np.outer(k, np.arange(cells_r)) % cells_r / cells_r
        radial = radial.reshape(modes // NEAR, NEAR, cells_r).transpose(1, 0, 2).reshape(modes, cells_r)
        group_l = cells_l // GROUPS
        axial = np.outer(k, np.arange(group_l)) % total_l / total_l
        angle = 2.0 * np.pi * (radial[:, None, None, :] + axial[None, :, :, None])
        angle = angle.reshape(modes * modes, group_l * cells_r)
        self.cells = np.stack(split_table(np.concatenate([np.cos(angle), -np.sin(angle)], 0)))
        angle = 2.0 * np.pi * (np.outer(np.arange(GROUPS) * group_l, k) % total_l / total_l)
        both = np.stack([np.cos(angle), np.sin(angle)], 1).astype(np.float32)
        self.rows = np.repeat(both[:, :, :, None], 128, 3)
        self.cols = np.tile(both, (1, 1, modes))[:, :, None, :]
        half = chans // 2
        angle = 2.0 * np.pi * np.outer(np.arange(cells_a), k) / total_a
        same = np.eye(half)

        def spread(table):
            whole = table[None, :, :, None] * same[:, None, None, :]
            return whole.reshape(half * cells_a, modes * half)

        self.turn = np.stack(split_table(spread(np.cos(angle))) + split_table(spread(np.sin(angle))))
        loc_a = modes // n_axial
        axial = (np.outer(np.arange(n_axial) * cells_l, k) % total_l / total_l).reshape(1, n_axial, modes, 1)
        azim = (np.outer(np.arange(n_azim) * cells_a, k) % total_a / total_a).reshape(n_azim, n_axial, 1, loc_a, 1)
        azim = np.broadcast_to(azim, (n_azim, n_axial, 2, loc_a, half)).reshape(n_azim, 1, 1, modes * chans)
        angle = 2.0 * np.pi * (axial + azim)
        self.place = np.stack([np.cos(angle), np.sin(angle)], 2).astype(np.float32)


def azimuth_analysis(values, turn, place, out_ref):
    cos_h, cos_l, sin_h, sin_l = (turn[i] for i in range(4))
    rows, cols = values.shape[0] // 2, values.shape[1] // 2
    near, groups, far, block, lanes = out_ref.shape
    n_kl = block // 2
    reals, imags = [], []
    for h in range(2):
        high, low = split(values[:, h * cols : (h + 1) * cols])
        by_cos = dot(high, cos_h) + dot(low, cos_h) + dot(high, cos_l)
        by_sin = dot(high, sin_h) + dot(low, sin_h) + dot(high, sin_l)
        reals.append(by_cos[:rows] + by_sin[rows:])
        imags.append(by_cos[rows:] - by_sin[:rows])
    for g in range(groups):
        at = slice(g * lanes // 2, (g + 1) * lanes // 2)
        re = jnp.concatenate([r[:, at] for r in reals], 1).reshape(near, far, n_kl, lanes)
        im = jnp.concatenate([i[:, at] for i in imags], 1).reshape(near, far, n_kl, lanes)
        to = slice(g * lanes, (g + 1) * lanes)
        c, s = place[0, :, to], place[1, :, to]
        out_ref[:, g, :, :n_kl, :] = re * c + im * s
        out_ref[:, g, :, n_kl:, :] = im * c - re * s


def azimuth_synthesis(mixed, turn, place, synth):
    near, groups, far, block, lanes = mixed.shape
    n_kl = block // 2
    rows = near * far * n_kl
    reals, imags = [], []
    for g in range(groups):
        re, im = mixed[:, g, :, :n_kl, :], mixed[:, g, :, n_kl:, :]
        to = slice(g * lanes, (g + 1) * lanes)
        c, s = place[0, :, to], place[1, :, to]
        reals.append((re * c - im * s).reshape(rows, lanes))
        imags.append((im * c + re * s).reshape(rows, lanes))
    cos_h, cos_l, sin_h, sin_l = (turn[i] for i in range(4))

    def times(t_h, t_l, v):
        return dot_nt(t_h, v[0]) + dot_nt(t_h, v[1]) + dot_nt(t_l, v[0])

    half = synth.shape[0] // 2
    for h in range(2):
        at = slice(h * lanes // 2, (h + 1) * lanes // 2)
        re = split(jnp.concatenate([r[:, at] for r in reals], 1))
        im = split(jnp.concatenate([i[:, at] for i in imags], 1))
        real = times(cos_h, cos_l, re) - times(sin_h, sin_l, im)
        imag = times(sin_h, sin_l, re) + times(cos_h, cos_l, im)
        synth[h * half : (h + 1) * half, :rows] = real
        synth[h * half : (h + 1) * half, rows:] = imag


def add_group(total, part, group, rows):
    if group == 0:
        return part
    half, cols = part.shape[0] // 2, part.shape[1]
    n_kl = rows.shape[2]
    re, im = part[:half].reshape(-1, n_kl, cols), part[half:].reshape(-1, n_kl, cols)
    c, s = rows[group, 0][:, :1], rows[group, 1][:, :1]
    turned = jnp.concatenate([re * c + im * s, im * c - re * s], 0)
    return total + turned.reshape(part.shape)


def turn_group(values, group, cols):
    if group == 0:
        return split(values)
    half = values.shape[1] // 2
    re, im = values[:, :half], values[:, half:]
    c, s = cols[group, 0], cols[group, 1]
    return split(jnp.concatenate([re * c - im * s, im * c + re * s], 1))


def start_columns(source, target, sems, widths):
    step = source.shape[1] // sum(widths)
    copies, at = [], 0
    for i, width in enumerate(widths):
        columns = pl.ds(at * step, width * step)
        copies.append(pltpu.make_async_copy(source.at[:, columns], target.at[:, columns], sems.at[i]))
        copies[-1].start()
        at += width
    return copies


def analysis_kernel(
    field, cells, turn, place, rows, cols, out, cells_here, turn_here, place_here, rows_here, cols_here, x, sems, more_sems
):
    y = lax.axis_index("axial")
    z = lax.axis_index("zh") * NEAR + lax.axis_index("zl")
    pairs = (
        (cells.at[0], cells_here.at[0]),
        (cells.at[1], cells_here.at[1]),
        (rows, rows_here),
        (turn, turn_here),
        (place.at[z, y], place_here),
        (cols, cols_here),
    )
    more = [pltpu.make_async_copy(a, b, more_sems.at[i]) for i, (a, b) in enumerate(pairs)]
    for copy in more[:3]:
        copy.start()
    first, rest = start_columns(field, x, sems, (1, GROUPS - 1))
    for copy in more[3:]:
        copy.start()
    step = x.shape[1] // GROUPS
    total = None
    for copy in (first, *more[:3]):
        copy.wait()
    for g in range(GROUPS):
        if g == 1:
            for copy in (rest, *more[3:]):
                copy.wait()
        values = x[:, g * step : (g + 1) * step]
        part = dot_nt(cells_here[0], values) + dot_nt(cells_here[1], values)
        total = add_group(total, part, g, rows_here)
    azimuth_analysis(total, turn_here, place_here, out)


def layer_kernel(
    mixed, cells, turn, place, rows, cols, local_far, cot_far, out, synth, pre, delta_h, delta_l, local, cot, sems
):
    copies = [pltpu.make_async_copy(local_far, local, sems.at[0]), pltpu.make_async_copy(cot_far, cot, sems.at[1])]
    for copy in copies:
        copy.start()
    azimuth_synthesis(mixed, turn, place, synth)
    step = local.shape[1] // GROUPS
    slope = math.sqrt(2.0 / math.pi)

    def synthesize(g):
        high, low = turn_group(synth[...], g, cols)
        pre[g] = dot(high, cells[0]) + dot(low, cells[0]) + dot(high, cells[1])

    def activate(g):
        at = slice(g * step, (g + 1) * step)
        value = pre[g] + local[:, at]
        square = value * value
        t = jnp.tanh(value * (slope + (slope * 0.044715) * square))
        inner = slope + (3.0 * slope * 0.044715) * square
        grad = 0.5 * (1.0 + t) + (0.5 * value) * (1.0 - t * t) * inner
        delta_h[g], delta_l[g] = split(cot[:, at].astype(F32) * grad)

    def analyze(g, total):
        high = delta_h[g]
        part = dot_nt(cells[0], high) + dot_nt(cells[0], delta_l[g]) + dot_nt(cells[1], high)
        return add_group(total, part, g, rows)

    ahead = 2
    for g in range(ahead):
        synthesize(g)
    for copy in copies:
        copy.wait()
    total = None
    for g in range(GROUPS):
        if ahead <= g + 1 < GROUPS:
            synthesize(g + 1)
        activate(g)
        if g > 0:
            total = analyze(g - 1, total)
    total = analyze(GROUPS - 1, total)
    azimuth_analysis(total, turn, place, out)


def prepare_kernel(
    weight_far, point_far, bias_far, field, out_weight, local_far, weight, point, bias, x, local, sems, chunk_sems, out_sems
):
    small = ((point_far, point), (bias_far, bias), (weight_far, weight))
    copies = [pltpu.make_async_copy(a, b, sems.at[i]) for i, (a, b) in enumerate(small)]
    for copy in copies:
        copy.start()
    chunks = start_columns(field, x, chunk_sems, (1,) * LOCAL_CHUNKS)
    step = x.shape[1] // LOCAL_CHUNKS
    n_q, n_ka, n_kl, chans, _ = weight.shape
    rows = x.shape[0]
    cells = rows // chans

    def owner(shape, axis):
        i, c = lax.broadcasted_iota(jnp.int32, shape, axis), lax.broadcasted_iota(jnp.int32, shape, 1 - axis)
        return (i >= c * cells) & (i < (c + 1) * cells)

    left = owner((rows, chans), 0)
    right = jnp.where(owner((chans, rows), 1), 1.0, 0.0).astype(BF)
    i = lax.broadcasted_iota(jnp.int32, (rows, rows), 0)
    j = lax.broadcasted_iota(jnp.int32, (rows, rows), 1)
    copies[0].wait()
    copies[1].wait()
    wide = dot(dot(jnp.where(left, 1.0, 0.0).astype(BF), point[...]).astype(BF), right)
    mix = jnp.where(i % cells == j % cells, wide, 0.0).astype(BF)
    shift = jnp.sum(jnp.where(left, bias[...], 0.0), 1, keepdims=True)
    sends = []
    for i in range(LOCAL_CHUNKS):
        chunks[i].wait()
        at = slice(i * step, (i + 1) * step)
        local[:, at] = dot(mix, x[:, at]) + shift
        to = pl.ds(i * step, step)
        sends.append(pltpu.make_async_copy(local.at[:, to], local_far.at[:, to], out_sems.at[i]))
        sends[-1].start()
    half = chans // 2
    lanes = n_ka * chans
    o = lax.broadcasted_iota(jnp.int32, (chans, lanes), 0)
    lane = lax.broadcasted_iota(jnp.int32, (chans, lanes), 1)
    copies[2].wait()
    for ka in range(n_ka):
        to = jnp.where(o < half, o, o + (n_ka - 1) * half) + ka * half
        place = jnp.where(lane == to, 1.0, 0.0).astype(BF)
        for q in range(n_q):
            moved = dot(weight[q, ka].reshape(n_kl * chans, chans), place).astype(BF)
            moved = moved.reshape(n_kl, 2, half, lanes)
            for h in range(2):
                at = h * lanes // 2 + ka * half
                out_weight[:, at : at + half, q * lanes : (q + 1) * lanes] = moved[:, h]
    for copy in sends:
        copy.wait()


def mix_kernel(scale, out_scale, parts, weight, spec, out):
    far, rows, lanes = parts.shape
    n_kl = rows // 2
    total = parts[0]
    for z in range(1, far):
        total = total + parts[z]
    total = total * scale
    spec[...] = total
    stack = jnp.concatenate([*split3(total[:n_kl]), *split3(total[n_kl:])], 0)
    row = lax.broadcasted_iota(jnp.int32, (stack.shape[0], 2 * lanes), 0) % n_kl
    got = jnp.zeros((stack.shape[0], 2 * lanes), F32)
    for kl in range(n_kl):
        got = jnp.where(row == kl, dot(stack, weight[kl]), got)
    by_re = got[:n_kl] + got[n_kl : 2 * n_kl] + got[2 * n_kl : 3 * n_kl]
    by_im = got[3 * n_kl : 4 * n_kl] + got[4 * n_kl : 5 * n_kl] + got[5 * n_kl :]
    re = (by_re[:, :lanes] - by_im[:, lanes:]) * out_scale
    im = (by_re[:, lanes:] + by_im[:, :lanes]) * out_scale
    for z in range(far):
        out[z, :n_kl, :] = re
        out[z, n_kl:, :] = im


def join_kernel(scale, parts, spec, out):
    far, rows, _ = parts.shape
    total = parts[0]
    for z in range(1, far):
        total = total + parts[z]
    total = total * scale
    for d in range(out.shape[0]):
        out[d, :rows, :] = spec[...]
        out[d, rows:, :] = total


def grad_kernel(pairs, out_far, out, sems):
    _, n_ka, n_kl, chans, _ = out.shape
    half = chans // 2
    lanes = pairs.shape[2]
    copies = []
    part = n_kl // sems.shape[0]
    for kl in range(n_kl):
        s_re, s_im, d_re, d_im = (pairs[:, i * n_kl + kl, :] for i in range(4))
        s_h, s_l = split(jnp.concatenate([s_re, s_im], 0))
        a = jnp.concatenate([d_re, d_im], 0)
        b = jnp.concatenate([d_im, -d_re], 0)
        d_h, d_l = split(jnp.concatenate([a, b], 1))
        left = jnp.concatenate([s_h, s_l, s_h], 0)
        right = jnp.concatenate([d_h, d_h, d_l], 0)
        whole = dot_tn(left, right)
        for q in range(2):
            for ka in range(n_ka):
                for h in range(2):
                    r = h * lanes // 2 + ka * half
                    for g in range(2):
                        c = q * lanes + g * lanes // 2 + ka * half
                        out[q, ka, kl, h * half : (h + 1) * half, g * half : (g + 1) * half] = whole[r : r + half, c : c + half]
        if kl % part == part - 1:
            at = pl.ds(kl + 1 - part, part)
            copies.append(pltpu.make_async_copy(out.at[:, :, at], out_far.at[:, :, at], sems.at[kl // part]))
            copies[-1].start()
    for copy in copies:
        copy.wait()


def call(kernel, out_shape, *args, **more):
    return pl.pallas_call(
        kernel,
        out_shape=out_shape,
        compiler_params=pltpu.CompilerParams(vmem_limit_bytes=VMEM),
        **more,
    )(*args)


def shape(*dims, dtype=F32):
    return jax.ShapeDtypeStruct(dims, dtype)


def per_device(field, cotangent, spectral_weight, point_weight, bias):
    _, chans, cells_a, merged = field.shape
    cells_r = NR
    cells_l = merged // cells_r
    far, n_axial, n_dp = (lax.axis_size(name) for name in ("zh", "axial", "dp"))
    n_azim = far * NEAR
    _, _, loc_a, modes, _, _ = spectral_weight.shape
    tables = Tables(modes, chans, cells_a, cells_l, cells_r, n_azim, n_axial)
    total_cells = cells_a * n_azim * cells_l * n_axial * cells_r
    forward_scale = 1.0 / math.sqrt(total_cells)
    mode_scale = 1.0 / (modes * math.sqrt(modes))
    rows_x = chans * cells_a
    rows_k = 2 * modes * modes
    lanes = loc_a * chans
    block = (2 * modes, lanes)
    whole = (NEAR, n_axial, far, *block)
    held = [jnp.asarray(t) for t in (tables.cells, tables.turn, tables.place, tables.rows, tables.cols)]
    x = field.reshape(rows_x, merged)
    cot = cotangent.reshape(rows_x, merged)
    near_axes = ("zl", "axial")

    def exchange(values, axes):
        flat = values.reshape(-1, *block)
        return lax.all_to_all(flat, axes, 0, 0, tiled=True).reshape(values.shape)

    def reduce(values):
        return exchange(exchange(values, near_axes).sum((0, 1)), "zh")

    far_off = pl.BlockSpec(memory_space=pl.ANY)
    near_by = pl.BlockSpec(memory_space=pltpu.VMEM)

    def stay(array):
        return pltpu.with_memory_space_constraint(array, pltpu.HBM)

    field_shape = pltpu.VMEM((rows_x, merged), BF)
    local_shape = pltpu.VMEM((rows_x, merged), F32)
    x, cot, *held = map(stay, (x, cot, *held))
    held_shapes = [pltpu.VMEM(t.shape[2:] if i == 2 else t.shape, t.dtype) for i, t in enumerate(held)]
    first, *held = call(
        analysis_kernel,
        (pltpu.VMEM(whole, F32), *held_shapes),
        x,
        *held,
        in_specs=[far_off] * 6,
        out_specs=[near_by] * 6,
        scratch_shapes=[
            field_shape,
            pltpu.SemaphoreType.DMA((2,)),
            pltpu.SemaphoreType.DMA((6,)),
        ],
    )
    weight_shape = spectral_weight[:, 0].shape
    weight, local = call(
        prepare_kernel,
        (pltpu.VMEM((modes, lanes, 2 * lanes), BF), pltpu.HBM((rows_x, merged), F32)),
        *map(stay, (spectral_weight[:, 0], point_weight, bias[None], x)),
        in_specs=[far_off] * 4,
        out_specs=[near_by, far_off],
        scratch_shapes=[
            pltpu.VMEM(weight_shape, BF),
            pltpu.VMEM(point_weight.shape, BF),
            pltpu.VMEM((1, chans), F32),
            field_shape,
            local_shape,
            pltpu.SemaphoreType.DMA((3,)),
            pltpu.SemaphoreType.DMA((LOCAL_CHUNKS,)),
            pltpu.SemaphoreType.DMA((LOCAL_CHUNKS,)),
        ],
    )
    parts = reduce(first)

    def mix_body(*refs):
        mix_kernel(forward_scale, mode_scale, *refs)

    spec, mixed = call(mix_body, (shape(*block), shape(far, *block)), parts, weight)
    mixed = exchange(mixed, "zh")
    mixed = exchange(jnp.broadcast_to(mixed, whole), near_axes)
    group = (GROUPS, rows_x, merged // GROUPS)
    second = call(
        layer_kernel,
        pltpu.VMEM(whole, F32),
        mixed,
        *held,
        stay(local),
        cot,
        in_specs=[near_by] * 6 + [far_off] * 2,
        out_specs=near_by,
        scratch_shapes=[
            pltpu.VMEM((rows_x, rows_k), F32),
            pltpu.VMEM(group, F32),
            pltpu.VMEM(group, BF),
            pltpu.VMEM(group, BF),
            local_shape,
            field_shape,
            pltpu.SemaphoreType.DMA((2,)),
        ],
    )
    parts = reduce(second)

    def join_body(*refs):
        join_kernel(mode_scale, *refs)

    pairs = call(join_body, shape(n_dp, 2 * block[0], lanes), parts, spec)
    pairs = lax.all_to_all(pairs, "dp", 0, 0, tiled=True)
    grad_dims = (2, loc_a, modes, chans, chans)
    grad = call(
        grad_kernel,
        pltpu.HBM(grad_dims, F32),
        pairs,
        in_specs=[near_by],
        out_specs=far_off,
        scratch_shapes=[pltpu.VMEM(grad_dims, F32), pltpu.SemaphoreType.DMA((4,))],
    )
    return grad[:, None]


def solution(mesh):
    n_dp, n_azim, n_axial = (mesh.shape[name] for name in ("dp", "azim", "axial"))
    fine = Mesh(mesh.devices.reshape(n_dp, n_azim // NEAR, NEAR, n_axial), ("dp", "zh", "zl", "axial"))
    azim = ("zh", "zl")
    in_specs = (
        P("dp", None, azim, "axial"),
        P("dp", None, azim, "axial"),
        P(None, azim, "axial", None, None, None),
        P(),
        P(),
    )
    out_specs = P(None, azim, "axial", None, None, None)
    return jax.shard_map(
        per_device, mesh=fine, in_specs=in_specs, out_specs=out_specs, check_vma=False
    )
```

```python
import math

import jax
import jax.numpy as jnp
import ml_dtypes
import numpy as np
from jax import lax
from jax.experimental import pallas as pl
from jax.experimental.pallas import tpu as pltpu
from jax.sharding import Mesh
from jax.sharding import PartitionSpec as P

NR = 64
NEAR = 2
BF = jnp.bfloat16
F32 = jnp.float32
GROUPS = 4
VMEM = 32 * 1024 * 1024


def split_table(values):
    high = values.astype(ml_dtypes.bfloat16)
    low = (values - high.astype(np.float64)).astype(ml_dtypes.bfloat16)
    return high, low


def split(values):
    high = values.astype(BF)
    return high, (values - high.astype(F32)).astype(BF)


def split3(values):
    high = values.astype(BF)
    rest = values - high.astype(F32)
    mid = rest.astype(BF)
    return high, mid, (rest - mid.astype(F32)).astype(BF)


def dot(a, b):
    return lax.dot_general(a, b, (((1,), (0,)), ((), ())), preferred_element_type=F32)


def dot_nt(a, b):
    return lax.dot_general(a, b, (((1,), (1,)), ((), ())), preferred_element_type=F32)


def dot_tn(a, b):
    return lax.dot_general(a, b, (((0,), (0,)), ((), ())), preferred_element_type=F32)


class Tables:
    def __init__(self, modes, chans, cells_a, cells_l, cells_r, n_azim, n_axial):
        total_a, total_l = cells_a * n_azim, cells_l * n_axial
        k = np.arange(modes)
        radial = np.outer(k, np.arange(cells_r)) % cells_r / cells_r
        radial = radial.reshape(modes // NEAR, NEAR, cells_r).transpose(1, 0, 2).reshape(modes, cells_r)
        group_l = cells_l // GROUPS
        axial = np.outer(k, np.arange(group_l)) % total_l / total_l
        angle = 2.0 * np.pi * (radial[:, None, None, :] + axial[None, :, :, None])
        angle = angle.reshape(modes * modes, group_l * cells_r)
        self.cells = np.stack(split_table(np.concatenate([np.cos(angle), -np.sin(angle)], 0)))
        angle = 2.0 * np.pi * (np.outer(np.arange(GROUPS) * group_l, k) % total_l / total_l)
        both = np.stack([np.cos(angle), np.sin(angle)], 1).astype(np.float32)
        self.rows = np.repeat(both[:, :, :, None], 128, 3)
        self.cols = np.tile(both, (1, 1, modes))[:, :, None, :]
        half = chans // 2
        angle = 2.0 * np.pi * np.outer(np.arange(cells_a), k) / total_a
        same = np.eye(half)

        def spread(table):
            whole = table[None, :, :, None] * same[:, None, None, :]
            return whole.reshape(half * cells_a, modes * half)

        self.turn = np.stack(split_table(spread(np.cos(angle))) + split_table(spread(np.sin(angle))))
        loc_a = modes // n_axial
        axial = (np.outer(np.arange(n_axial) * cells_l, k) % total_l / total_l).reshape(1, n_axial, modes, 1)
        azim = (np.outer(np.arange(n_azim) * cells_a, k) % total_a / total_a).reshape(n_azim, n_axial, 1, loc_a, 1)
        azim = np.broadcast_to(azim, (n_azim, n_axial, 2, loc_a, half)).reshape(n_azim, 1, 1, modes * chans)
        angle = 2.0 * np.pi * (axial + azim)
        self.place = np.stack([np.cos(angle), np.sin(angle)], 2).astype(np.float32)


def azimuth_analysis(values, turn, place, out_ref):
    cos_h, cos_l, sin_h, sin_l = (turn[i] for i in range(4))
    rows, cols = values.shape[0] // 2, values.shape[1] // 2
    near, groups, far, block, lanes = out_ref.shape
    n_kl = block // 2
    reals, imags = [], []
    for h in range(2):
        high, low = split(values[:, h * cols : (h + 1) * cols])
        by_cos = dot(high, cos_h) + dot(low, cos_h) + dot(high, cos_l)
        by_sin = dot(high, sin_h) + dot(low, sin_h) + dot(high, sin_l)
        reals.append(by_cos[:rows] + by_sin[rows:])
        imags.append(by_cos[rows:] - by_sin[:rows])
    for g in range(groups):
        at = slice(g * lanes // 2, (g + 1) * lanes // 2)
        re = jnp.concatenate([r[:, at] for r in reals], 1).reshape(near, far, n_kl, lanes)
        im = jnp.concatenate([i[:, at] for i in imags], 1).reshape(near, far, n_kl, lanes)
        to = slice(g * lanes, (g + 1) * lanes)
        c, s = place[0, :, to], place[1, :, to]
        out_ref[:, g, :, :n_kl, :] = re * c + im * s
        out_ref[:, g, :, n_kl:, :] = im * c - re * s


def azimuth_synthesis(mixed, turn, place, synth):
    near, groups, far, block, lanes = mixed.shape
    n_kl = block // 2
    rows = near * far * n_kl
    reals, imags = [], []
    for g in range(groups):
        re, im = mixed[:, g, :, :n_kl, :], mixed[:, g, :, n_kl:, :]
        to = slice(g * lanes, (g + 1) * lanes)
        c, s = place[0, :, to], place[1, :, to]
        reals.append((re * c - im * s).reshape(rows, lanes))
        imags.append((im * c + re * s).reshape(rows, lanes))
    cos_h, cos_l, sin_h, sin_l = (turn[i] for i in range(4))

    def times(t_h, t_l, v):
        return dot_nt(t_h, v[0]) + dot_nt(t_h, v[1]) + dot_nt(t_l, v[0])

    half = synth.shape[0] // 2
    for h in range(2):
        at = slice(h * lanes // 2, (h + 1) * lanes // 2)
        re = split(jnp.concatenate([r[:, at] for r in reals], 1))
        im = split(jnp.concatenate([i[:, at] for i in imags], 1))
        real = times(cos_h, cos_l, re) - times(sin_h, sin_l, im)
        imag = times(sin_h, sin_l, re) + times(cos_h, cos_l, im)
        synth[h * half : (h + 1) * half, :rows] = real
        synth[h * half : (h + 1) * half, rows:] = imag


def add_group(total, part, group, rows):
    if group == 0:
        return part
    half, cols = part.shape[0] // 2, part.shape[1]
    n_kl = rows.shape[2]
    re, im = part[:half].reshape(-1, n_kl, cols), part[half:].reshape(-1, n_kl, cols)
    c, s = rows[group, 0][:, :1], rows[group, 1][:, :1]
    turned = jnp.concatenate([re * c + im * s, im * c - re * s], 0)
    return total + turned.reshape(part.shape)


def turn_group(values, group, cols):
    if group == 0:
        return split(values)
    half = values.shape[1] // 2
    re, im = values[:, :half], values[:, half:]
    c, s = cols[group, 0], cols[group, 1]
    return split(jnp.concatenate([re * c - im * s, im * c + re * s], 1))


def start_columns(source, target, sems, widths):
    step = source.shape[1] // sum(widths)
    copies, at = [], 0
    for i, width in enumerate(widths):
        columns = pl.ds(at * step, width * step)
        copies.append(pltpu.make_async_copy(source.at[:, columns], target.at[:, columns], sems.at[i]))
        copies[-1].start()
        at += width
    return copies


def analysis_kernel(
    field, cells, turn, place, rows, cols, point_far, bias_far,
    out, cells_here, turn_here, place_here, rows_here, cols_here, out_mix, out_bias, x, point, bias, sems, more_sems,
):
    y = lax.axis_index("axial")
    z = lax.axis_index("zh") * NEAR + lax.axis_index("zl")
    pairs = (
        (point_far, point),
        (bias_far, bias),
        (cells.at[0], cells_here.at[0]),
        (cells.at[1], cells_here.at[1]),
        (rows, rows_here),
        (turn, turn_here),
        (place.at[z, y], place_here),
        (cols, cols_here),
    )
    more = [pltpu.make_async_copy(a, b, more_sems.at[i]) for i, (a, b) in enumerate(pairs)]
    for copy in more[:5]:
        copy.start()
    first, rest = start_columns(field, x, sems, (1, GROUPS - 1))
    for copy in more[5:]:
        copy.start()
    step = x.shape[1] // GROUPS
    total = None
    for copy in more[:2]:
        copy.wait()
    spread_rows(point, bias, out_mix, out_bias)
    for copy in (first, *more[2:5]):
        copy.wait()
    for g in range(GROUPS):
        if g == 1:
            for copy in (rest, *more[5:]):
                copy.wait()
        values = x[:, g * step : (g + 1) * step]
        part = dot_nt(cells_here[0], values) + dot_nt(cells_here[1], values)
        total = add_group(total, part, g, rows_here)
    azimuth_analysis(total, turn_here, place_here, out)


def layer_kernel(
    mixed, cells, turn, place, rows, cols, mix, bias, field, cot_far, out, synth, pre, delta_h, delta_l, x, cot, sems
):
    copies = [pltpu.make_async_copy(field, x, sems.at[0]), pltpu.make_async_copy(cot_far, cot, sems.at[1])]
    for copy in copies:
        copy.start()
    azimuth_synthesis(mixed, turn, place, synth)
    step = x.shape[1] // GROUPS
    shift = jnp.concatenate([bias[...]] * (step // bias.shape[1]), 1)
    slope = math.sqrt(2.0 / math.pi)

    def synthesize(g):
        high, low = turn_group(synth[...], g, cols)
        pre[g] = dot(high, cells[0]) + dot(low, cells[0]) + dot(high, cells[1])

    def activate(g):
        at = slice(g * step, (g + 1) * step)
        value = pre[g] + dot(mix[...], x[:, at]) + shift
        square = value * value
        t = jnp.tanh(value * (slope + (slope * 0.044715) * square))
        inner = slope + (3.0 * slope * 0.044715) * square
        grad = 0.5 * (1.0 + t) + (0.5 * value) * (1.0 - t * t) * inner
        delta_h[g], delta_l[g] = split(cot[:, at].astype(F32) * grad)

    def analyze(g, total):
        high = delta_h[g]
        part = dot_nt(cells[0], high) + dot_nt(cells[0], delta_l[g]) + dot_nt(cells[1], high)
        return add_group(total, part, g, rows)

    ahead = 2
    for g in range(ahead):
        synthesize(g)
    for copy in copies:
        copy.wait()
    total = None
    for g in range(GROUPS):
        if ahead <= g + 1 < GROUPS:
            synthesize(g + 1)
        activate(g)
        if g > 0:
            total = analyze(g - 1, total)
    total = analyze(GROUPS - 1, total)
    azimuth_analysis(total, turn, place, out)


def spread_rows(point, bias, out_mix, out_bias):
    chans, rows = point.shape[0], out_mix.shape[0]
    cells = rows // chans

    def owner(shape, axis):
        i, c = lax.broadcasted_iota(jnp.int32, shape, axis), lax.broadcasted_iota(jnp.int32, shape, 1 - axis)
        return (i >= c * cells) & (i < (c + 1) * cells)

    left = owner((rows, chans), 0)
    right = jnp.where(owner((chans, rows), 1), 1.0, 0.0).astype(BF)
    wide = dot(dot(jnp.where(left, 1.0, 0.0).astype(BF), point[...]).astype(BF), right)
    i = lax.broadcasted_iota(jnp.int32, (rows, rows), 0)
    j = lax.broadcasted_iota(jnp.int32, (rows, rows), 1)
    out_mix[...] = jnp.where(i % cells == j % cells, wide, 0.0).astype(BF)
    column = jnp.sum(jnp.where(left, bias[...], 0.0), 1, keepdims=True)
    out_bias[...] = jnp.broadcast_to(column, out_bias.shape)


def pack_weights(weight, out):
    n_q, n_ka, n_kl, chans, _ = weight.shape
    half = chans // 2
    lanes = n_ka * chans
    o = lax.broadcasted_iota(jnp.int32, (chans, lanes), 0)
    lane = lax.broadcasted_iota(jnp.int32, (chans, lanes), 1)
    for ka in range(n_ka):
        to = jnp.where(o < half, o, o + (n_ka - 1) * half) + ka * half
        place = jnp.where(lane == to, 1.0, 0.0).astype(BF)
        for q in range(n_q):
            moved = dot(weight[q, ka].reshape(n_kl * chans, chans), place).astype(BF)
            moved = moved.reshape(n_kl, 2, half, lanes)
            for h in range(2):
                at = h * lanes // 2 + ka * half
                out[:, at : at + half, q * lanes : (q + 1) * lanes] = moved[:, h]


def sum_kernel(parts, out):
    near, groups, *_ = parts.shape
    total = None
    for place in range(near * groups):
        part = parts[place // groups, place % groups]
        total = part if total is None else total + part
    out[...] = total


def mix_kernel(scale, out_scale, parts, raw, spec, out, weight):
    pack_weights(raw, weight)
    far, rows, lanes = parts.shape
    n_kl = rows // 2
    total = parts[0]
    for z in range(1, far):
        total = total + parts[z]
    total = total * scale
    spec[...] = total
    stack = jnp.concatenate([*split3(total[:n_kl]), *split3(total[n_kl:])], 0)
    row = lax.broadcasted_iota(jnp.int32, (stack.shape[0], 2 * lanes), 0) % n_kl
    got = jnp.zeros((stack.shape[0], 2 * lanes), F32)
    for kl in range(n_kl):
        got = jnp.where(row == kl, dot(stack, weight[kl]), got)
    by_re = got[:n_kl] + got[n_kl : 2 * n_kl] + got[2 * n_kl : 3 * n_kl]
    by_im = got[3 * n_kl : 4 * n_kl] + got[4 * n_kl : 5 * n_kl] + got[5 * n_kl :]
    re = (by_re[:, :lanes] - by_im[:, lanes:]) * out_scale
    im = (by_re[:, lanes:] + by_im[:, :lanes]) * out_scale
    for z in range(far):
        out[z, :n_kl, :] = re
        out[z, n_kl:, :] = im


def join_kernel(scale, parts, spec, out):
    far, rows, _ = parts.shape
    total = parts[0]
    for z in range(1, far):
        total = total + parts[z]
    total = total * scale
    for d in range(out.shape[0]):
        out[d, :rows, :] = spec[...]
        out[d, rows:, :] = total


def grad_kernel(pairs, out_far, out, sems):
    _, n_ka, n_kl, chans, _ = out.shape
    half = chans // 2
    lanes = pairs.shape[2]
    copies = []
    part = n_kl // sems.shape[0]
    for kl in range(n_kl):
        s_re, s_im, d_re, d_im = (pairs[:, i * n_kl + kl, :] for i in range(4))
        s_h, s_l = split(jnp.concatenate([s_re, s_im], 0))
        a = jnp.concatenate([d_re, d_im], 0)
        b = jnp.concatenate([d_im, -d_re], 0)
        d_h, d_l = split(jnp.concatenate([a, b], 1))
        left = jnp.concatenate([s_h, s_l, s_h], 0)
        right = jnp.concatenate([d_h, d_h, d_l], 0)
        whole = dot_tn(left, right)
        for q in range(2):
            for ka in range(n_ka):
                for h in range(2):
                    r = h * lanes // 2 + ka * half
                    for g in range(2):
                        c = q * lanes + g * lanes // 2 + ka * half
                        out[q, ka, kl, h * half : (h + 1) * half, g * half : (g + 1) * half] = whole[r : r + half, c : c + half]
        if kl % part == part - 1:
            at = pl.ds(kl + 1 - part, part)
            copies.append(pltpu.make_async_copy(out.at[:, :, at], out_far.at[:, :, at], sems.at[kl // part]))
            copies[-1].start()
    for copy in copies:
        copy.wait()


def call(kernel, out_shape, *args, **more):
    return pl.pallas_call(
        kernel,
        out_shape=out_shape,
        compiler_params=pltpu.CompilerParams(vmem_limit_bytes=VMEM),
        **more,
    )(*args)


def shape(*dims, dtype=F32):
    return jax.ShapeDtypeStruct(dims, dtype)


def per_device(field, cotangent, spectral_weight, point_weight, bias):
    _, chans, cells_a, merged = field.shape
    cells_r = NR
    cells_l = merged // cells_r
    far, n_axial, n_dp = (lax.axis_size(name) for name in ("zh", "axial", "dp"))
    n_azim = far * NEAR
    _, _, loc_a, modes, _, _ = spectral_weight.shape
    tables = Tables(modes, chans, cells_a, cells_l, cells_r, n_azim, n_axial)
    total_cells = cells_a * n_azim * cells_l * n_axial * cells_r
    forward_scale = 1.0 / math.sqrt(total_cells)
    mode_scale = 1.0 / (modes * math.sqrt(modes))
    rows_x = chans * cells_a
    rows_k = 2 * modes * modes
    lanes = loc_a * chans
    block = (2 * modes, lanes)
    whole = (NEAR, n_axial, far, *block)
    held = [jnp.asarray(t) for t in (tables.cells, tables.turn, tables.place, tables.rows, tables.cols)]
    x = field.reshape(rows_x, merged)
    cot = cotangent.reshape(rows_x, merged)
    near_axes = ("zl", "axial")

    def exchange(values, axes):
        flat = values.reshape(-1, *block)
        return lax.all_to_all(flat, axes, 0, 0, tiled=True).reshape(values.shape)

    def reduce(values):
        return exchange(call(sum_kernel, pltpu.VMEM((far, *block), F32), exchange(values, near_axes)), "zh")

    far_off = pl.BlockSpec(memory_space=pl.ANY)
    near_by = pl.BlockSpec(memory_space=pltpu.VMEM)

    def stay(array):
        return pltpu.with_memory_space_constraint(array, pltpu.HBM)

    field_shape = pltpu.VMEM((rows_x, merged), BF)
    x, cot, *held = map(stay, (x, cot, *held))
    held_shapes = [pltpu.VMEM(t.shape[2:] if i == 2 else t.shape, t.dtype) for i, t in enumerate(held)]
    first, *held = call(
        analysis_kernel,
        (pltpu.VMEM(whole, F32), *held_shapes, pltpu.VMEM((rows_x, rows_x), BF), pltpu.VMEM((rows_x, 128), F32)),
        x,
        *held,
        stay(point_weight),
        stay(bias[None]),
        in_specs=[far_off] * 8,
        out_specs=[near_by] * 8,
        scratch_shapes=[
            field_shape,
            pltpu.VMEM(point_weight.shape, BF),
            pltpu.VMEM((1, chans), F32),
            pltpu.SemaphoreType.DMA((2,)),
            pltpu.SemaphoreType.DMA((8,)),
        ],
    )
    parts = reduce(first)

    def mix_body(*refs):
        mix_kernel(forward_scale, mode_scale, *refs)

    spec, mixed = call(
        mix_body,
        (shape(*block), shape(far, *block)),
        parts,
        spectral_weight[:, 0],
        scratch_shapes=[pltpu.VMEM((modes, lanes, 2 * lanes), BF)],
    )
    mixed = exchange(mixed, "zh")
    mixed = exchange(jnp.broadcast_to(mixed, whole), near_axes)
    group = (GROUPS, rows_x, merged // GROUPS)
    second = call(
        layer_kernel,
        pltpu.VMEM(whole, F32),
        mixed,
        *held,
        x,
        cot,
        in_specs=[near_by] * 8 + [far_off] * 2,
        out_specs=near_by,
        scratch_shapes=[
            pltpu.VMEM((rows_x, rows_k), F32),
            pltpu.VMEM(group, F32),
            pltpu.VMEM(group, BF),
            pltpu.VMEM(group, BF),
            field_shape,
            field_shape,
            pltpu.SemaphoreType.DMA((2,)),
        ],
    )
    parts = reduce(second)

    def join_body(*refs):
        join_kernel(mode_scale, *refs)

    pairs = call(join_body, shape(n_dp, 2 * block[0], lanes), parts, spec)
    pairs = lax.all_to_all(pairs, "dp", 0, 0, tiled=True)
    grad_dims = (2, loc_a, modes, chans, chans)
    grad = call(
        grad_kernel,
        pltpu.HBM(grad_dims, F32),
        pairs,
        in_specs=[near_by],
        out_specs=far_off,
        scratch_shapes=[pltpu.VMEM(grad_dims, F32), pltpu.SemaphoreType.DMA((4,))],
    )
    return grad[:, None]


def solution(mesh):
    n_dp, n_azim, n_axial = (mesh.shape[name] for name in ("dp", "azim", "axial"))
    fine = Mesh(mesh.devices.reshape(n_dp, n_azim // NEAR, NEAR, n_axial), ("dp", "zh", "zl", "axial"))
    azim = ("zh", "zl")
    in_specs = (
        P("dp", None, azim, "axial"),
        P("dp", None, azim, "axial"),
        P(None, azim, "axial", None, None, None),
        P(),
        P(),
    )
    out_specs = P(None, azim, "axial", None, None, None)
    return jax.shard_map(
        per_device, mesh=fine, in_specs=in_specs, out_specs=out_specs, check_vma=False
    )
```

```python
import math

import jax
import jax.numpy as jnp
import ml_dtypes
import numpy as np
from jax import lax
from jax.experimental import pallas as pl
from jax.experimental.pallas import tpu as pltpu
from jax.sharding import Mesh
from jax.sharding import PartitionSpec as P

NR = 64
NEAR = 2
BF = jnp.bfloat16
F32 = jnp.float32
GROUPS = 4
VMEM = 32 * 1024 * 1024


def split_table(values):
    high = values.astype(ml_dtypes.bfloat16)
    low = (values - high.astype(np.float64)).astype(ml_dtypes.bfloat16)
    return high, low


def split(values):
    high = values.astype(BF)
    return high, (values - high.astype(F32)).astype(BF)


def split3(values):
    high = values.astype(BF)
    rest = values - high.astype(F32)
    mid = rest.astype(BF)
    return high, mid, (rest - mid.astype(F32)).astype(BF)


def dot(a, b):
    return lax.dot_general(a, b, (((1,), (0,)), ((), ())), preferred_element_type=F32)


def dot_nt(a, b):
    return lax.dot_general(a, b, (((1,), (1,)), ((), ())), preferred_element_type=F32)


def dot_tn(a, b):
    return lax.dot_general(a, b, (((0,), (0,)), ((), ())), preferred_element_type=F32)


class Tables:
    def __init__(self, modes, chans, cells_a, cells_l, cells_r, n_azim, n_axial):
        total_a, total_l = cells_a * n_azim, cells_l * n_axial
        k = np.arange(modes)
        radial = np.outer(k, np.arange(cells_r)) % cells_r / cells_r
        radial = radial.reshape(modes // NEAR, NEAR, cells_r).transpose(1, 0, 2).reshape(modes, cells_r)
        group_l = cells_l // GROUPS
        axial = np.outer(k, np.arange(group_l)) % total_l / total_l
        angle = 2.0 * np.pi * (radial[:, None, None, :] + axial[None, :, :, None])
        angle = angle.reshape(modes * modes, group_l * cells_r)
        self.cells = np.stack(split_table(np.concatenate([np.cos(angle), -np.sin(angle)], 0)))
        order = np.arange(group_l).reshape(-1, 2, 2).transpose(0, 2, 1).reshape(-1)
        parted = self.cells.reshape(2, 2, NEAR, modes * modes // NEAR, group_l, 2, cells_r // 2)[..., order, 0, :]
        self.halves = parted.transpose(0, 2, 1, 3, 4, 5).reshape(2, NEAR, 2 * modes * modes // NEAR, group_l * cells_r // 2)
        angle = 2.0 * np.pi * (np.outer(np.arange(GROUPS) * group_l, k) % total_l / total_l)
        both = np.stack([np.cos(angle), np.sin(angle)], 1).astype(np.float32)
        self.rows = np.repeat(both[:, :, :, None], 128, 3)
        self.cols = np.tile(both, (1, 1, modes // NEAR))[:, :, None, :]
        half = chans // 2
        angle = 2.0 * np.pi * np.outer(np.arange(cells_a), k) / total_a
        same = np.eye(half)

        def spread(table):
            whole = table[None, :, :, None] * same[:, None, None, :]
            return whole.reshape(half * cells_a, modes * half)

        self.turn = np.stack(split_table(spread(np.cos(angle))) + split_table(spread(np.sin(angle))))
        loc_a = modes // n_axial
        axial = (np.outer(np.arange(n_axial) * cells_l, k) % total_l / total_l).reshape(1, n_axial, modes, 1)
        azim = (np.outer(np.arange(n_azim) * cells_a, k) % total_a / total_a).reshape(n_azim, n_axial, 1, loc_a, 1)
        azim = np.broadcast_to(azim, (n_azim, n_axial, 2, loc_a, half)).reshape(n_azim, 1, 1, modes * chans)
        angle = 2.0 * np.pi * (axial + azim)
        self.place = np.stack([np.cos(angle), np.sin(angle)], 2).astype(np.float32)


def azimuth_analysis(values, turn, place, out_ref):
    cos_h, cos_l, sin_h, sin_l = (turn[i] for i in range(4))
    rows, cols = values.shape[0] // 2, values.shape[1] // 2
    near, groups, far, block, lanes = out_ref.shape
    n_kl = block // 2
    reals, imags = [], []
    for h in range(2):
        high, low = split(values[:, h * cols : (h + 1) * cols])
        by_cos = dot(high, cos_h) + dot(low, cos_h) + dot(high, cos_l)
        by_sin = dot(high, sin_h) + dot(low, sin_h) + dot(high, sin_l)
        reals.append(by_cos[:rows] + by_sin[rows:])
        imags.append(by_cos[rows:] - by_sin[:rows])
    for g in range(groups):
        at = slice(g * lanes // 2, (g + 1) * lanes // 2)
        re = jnp.concatenate([r[:, at] for r in reals], 1).reshape(near, far, n_kl, lanes)
        im = jnp.concatenate([i[:, at] for i in imags], 1).reshape(near, far, n_kl, lanes)
        to = slice(g * lanes, (g + 1) * lanes)
        c, s = place[0, :, to], place[1, :, to]
        out_ref[:, g, :, :n_kl, :] = re * c + im * s
        out_ref[:, g, :, n_kl:, :] = im * c - re * s


def azimuth_synthesis(mixed, turn, place, synth):
    near, groups, far, block, lanes = mixed.shape
    n_kl = block // 2
    rows = near * far * n_kl
    reals, imags = [], []
    for g in range(groups):
        re, im = mixed[:, g, :, :n_kl, :], mixed[:, g, :, n_kl:, :]
        to = slice(g * lanes, (g + 1) * lanes)
        c, s = place[0, :, to], place[1, :, to]
        reals.append((re * c - im * s).reshape(rows, lanes))
        imags.append((im * c + re * s).reshape(rows, lanes))
    cos_h, cos_l, sin_h, sin_l = (turn[i] for i in range(4))

    def times(t_h, t_l, v):
        return dot_nt(t_h, v[0]) + dot_nt(t_h, v[1]) + dot_nt(t_l, v[0])

    half = synth.shape[0] // 2
    for h in range(2):
        at = slice(h * lanes // 2, (h + 1) * lanes // 2)
        re = split(jnp.concatenate([r[:, at] for r in reals], 1))
        im = split(jnp.concatenate([i[:, at] for i in imags], 1))
        real = times(cos_h, cos_l, re) - times(sin_h, sin_l, im)
        imag = times(sin_h, sin_l, re) + times(cos_h, cos_l, im)
        synth[h * half : (h + 1) * half, :rows] = real
        synth[h * half : (h + 1) * half, rows:] = imag


def add_group(total, part, group, rows):
    if group == 0:
        return part
    half, cols = part.shape[0] // 2, part.shape[1]
    n_kl = rows.shape[2]
    re, im = part[:half].reshape(-1, n_kl, cols), part[half:].reshape(-1, n_kl, cols)
    c, s = rows[group, 0][:, :1], rows[group, 1][:, :1]
    turned = jnp.concatenate([re * c + im * s, im * c - re * s], 0)
    return total + turned.reshape(part.shape)


def turn_group(values, group, cols):
    if group == 0:
        return split(values)
    half = values.shape[1] // 2
    re, im = values[:, :half], values[:, half:]
    c, s = cols[group, 0], cols[group, 1]
    return split(jnp.concatenate([re * c - im * s, im * c + re * s], 1))


def first_half():
    return lax.broadcasted_iota(jnp.int32, (1, 128), 1) % NR < NR // 2


def fold(values):
    a, b = values[:, :128], values[:, 128:]
    u = jnp.where(first_half(), a, pltpu.roll(b, NR // 2, 1))
    v = jnp.where(first_half(), pltpu.roll(a, 128 - NR // 2, 1), b)
    return u + v, u - v


def unfold(even, odd):
    u, v = even + odd, even - odd
    a = jnp.where(first_half(), u, pltpu.roll(v, NR // 2, 1))
    b = jnp.where(first_half(), pltpu.roll(u, 128 - NR // 2, 1), v)
    return a, b


def start_columns(source, target, sems, widths):
    step = source.shape[1] // sum(widths)
    copies, at = [], 0
    for i, width in enumerate(widths):
        columns = pl.ds(at * step, width * step)
        copies.append(pltpu.make_async_copy(source.at[:, columns], target.at[:, columns], sems.at[i]))
        copies[-1].start()
        at += width
    return copies


def analysis_kernel(
    field, halves, turn, place, rows, cols, cells, point_far, bias_far,
    out, halves_here, turn_here, place_here, rows_here, cols_here, out_mix, out_bias, x, cells_here, point, bias, sems, more_sems,
):
    y = lax.axis_index("axial")
    z = lax.axis_index("zh") * NEAR + lax.axis_index("zl")
    pairs = (
        (point_far, point),
        (bias_far, bias),
        (cells.at[0], cells_here.at[0]),
        (cells.at[1], cells_here.at[1]),
        (rows, rows_here),
        (turn, turn_here),
        (place.at[z, y], place_here),
        (cols, cols_here),
        (halves, halves_here),
    )
    more = [pltpu.make_async_copy(a, b, more_sems.at[i]) for i, (a, b) in enumerate(pairs)]
    for copy in more[:5]:
        copy.start()
    first, rest = start_columns(field, x, sems, (1, GROUPS - 1))
    for copy in more[5:]:
        copy.start()
    step = x.shape[1] // GROUPS
    total = None
    for copy in more[:2]:
        copy.wait()
    spread_rows(point, bias, out_mix, out_bias)
    for copy in (first, *more[2:5]):
        copy.wait()
    for g in range(GROUPS):
        if g == 1:
            for copy in (rest, *more[5:]):
                copy.wait()
        values = x[:, g * step : (g + 1) * step]
        part = dot_nt(cells_here[0], values) + dot_nt(cells_here[1], values)
        total = add_group(total, part, g, rows_here)
    azimuth_analysis(total, turn_here, place_here, out)


def layer_kernel(
    mixed, halves, turn, place, rows, cols, mix, bias, field, cot_far, out, synth, pre, delta_h, delta_l, x, cot, sems
):
    copies = [pltpu.make_async_copy(field, x, sems.at[0]), pltpu.make_async_copy(cot_far, cot, sems.at[1])]
    for copy in copies:
        copy.start()
    azimuth_synthesis(mixed, turn, place, synth)
    step = x.shape[1] // GROUPS
    shift = jnp.concatenate([bias[...]] * (step // bias.shape[1]), 1)
    slope = math.sqrt(2.0 / math.pi)

    half = synth.shape[1] // 2
    part = half // NEAR

    def synthesize(g):
        sums = []
        for p in range(NEAR):
            at = [synth[:, q * half + p * part : q * half + (p + 1) * part] for q in range(2)]
            high, low = turn_group(jnp.concatenate(at, 1), g, cols)
            sums.append(dot(high, halves[0, p]) + dot(low, halves[0, p]) + dot(high, halves[1, p]))
        for j in range(step // 256):
            a, b = unfold(*(value[:, j * 128 : (j + 1) * 128] for value in sums))
            pre[g, :, j * 256 : j * 256 + 128] = a
            pre[g, :, j * 256 + 128 : (j + 1) * 256] = b

    def activate(g):
        at = slice(g * step, (g + 1) * step)
        value = pre[g] + dot(mix[...], x[:, at]) + shift
        square = value * value
        t = jnp.tanh(value * (slope + (slope * 0.044715) * square))
        inner = slope + (3.0 * slope * 0.044715) * square
        grad = 0.5 * (1.0 + t) + (0.5 * value) * (1.0 - t * t) * inner
        delta = cot[:, at].astype(F32) * grad
        for j in range(step // 256):
            to = slice(j * 128, (j + 1) * 128)
            for p, value in enumerate(fold(delta[:, j * 256 : (j + 1) * 256])):
                delta_h[g, p, :, to], delta_l[g, p, :, to] = split(value)

    def analyze(g, totals):
        out = []
        for p in range(NEAR):
            high = delta_h[g, p]
            both = dot_nt(halves[:, p].reshape(2 * half, -1), high)
            value = both[:half] + both[half:] + dot_nt(halves[0, p], delta_l[g, p])
            out.append(add_group(totals[p], value, g, rows))
        return out

    ahead = 2
    for g in range(ahead):
        synthesize(g)
    for copy in copies:
        copy.wait()
    totals = [None] * NEAR
    for g in range(GROUPS):
        if ahead <= g + 1 < GROUPS:
            synthesize(g + 1)
        activate(g)
        if g > 0:
            totals = analyze(g - 1, totals)
    totals = analyze(GROUPS - 1, totals)
    total = jnp.concatenate([value[q * part : (q + 1) * part] for q in range(2) for value in totals], 0)
    azimuth_analysis(total, turn, place, out)


def spread_rows(point, bias, out_mix, out_bias):
    chans, rows = point.shape[0], out_mix.shape[0]
    cells = rows // chans

    def owner(shape, axis):
        i, c = lax.broadcasted_iota(jnp.int32, shape, axis), lax.broadcasted_iota(jnp.int32, shape, 1 - axis)
        return (i >= c * cells) & (i < (c + 1) * cells)

    left = owner((rows, chans), 0)
    right = jnp.where(owner((chans, rows), 1), 1.0, 0.0).astype(BF)
    wide = dot(dot(jnp.where(left, 1.0, 0.0).astype(BF), point[...]).astype(BF), right)
    i = lax.broadcasted_iota(jnp.int32, (rows, rows), 0)
    j = lax.broadcasted_iota(jnp.int32, (rows, rows), 1)
    out_mix[...] = jnp.where(i % cells == j % cells, wide, 0.0).astype(BF)
    column = jnp.sum(jnp.where(left, bias[...], 0.0), 1, keepdims=True)
    out_bias[...] = jnp.broadcast_to(column, out_bias.shape)


def pack_weights(weight, out):
    n_q, n_ka, n_kl, chans, _ = weight.shape
    half = chans // 2
    lanes = n_ka * chans
    o = lax.broadcasted_iota(jnp.int32, (chans, lanes), 0)
    lane = lax.broadcasted_iota(jnp.int32, (chans, lanes), 1)
    for ka in range(n_ka):
        to = jnp.where(o < half, o, o + (n_ka - 1) * half) + ka * half
        place = jnp.where(lane == to, 1.0, 0.0).astype(BF)
        for q in range(n_q):
            moved = dot(weight[q, ka].reshape(n_kl * chans, chans), place).astype(BF)
            moved = moved.reshape(n_kl, 2, half, lanes)
            for h in range(2):
                at = h * lanes // 2 + ka * half
                out[:, at : at + half, q * lanes : (q + 1) * lanes] = moved[:, h]


def sum_kernel(parts, out):
    near, groups, *_ = parts.shape
    total = None
    for place in range(near * groups):
        part = parts[place // groups, place % groups]
        total = part if total is None else total + part
    out[...] = total


def mix_kernel(scale, out_scale, parts, raw, spec, out, weight):
    pack_weights(raw, weight)
    far, rows, lanes = parts.shape
    n_kl = rows // 2
    total = parts[0]
    for z in range(1, far):
        total = total + parts[z]
    total = total * scale
    spec[...] = total
    stack = jnp.concatenate([*split3(total[:n_kl]), *split3(total[n_kl:])], 0)
    row = lax.broadcasted_iota(jnp.int32, (stack.shape[0], 2 * lanes), 0) % n_kl
    got = jnp.zeros((stack.shape[0], 2 * lanes), F32)
    for kl in range(n_kl):
        got = jnp.where(row == kl, dot(stack, weight[kl]), got)
    by_re = got[:n_kl] + got[n_kl : 2 * n_kl] + got[2 * n_kl : 3 * n_kl]
    by_im = got[3 * n_kl : 4 * n_kl] + got[4 * n_kl : 5 * n_kl] + got[5 * n_kl :]
    re = (by_re[:, :lanes] - by_im[:, lanes:]) * out_scale
    im = (by_re[:, lanes:] + by_im[:, :lanes]) * out_scale
    for z in range(far):
        out[z, :n_kl, :] = re
        out[z, n_kl:, :] = im


def join_kernel(scale, parts, spec, out):
    far, rows, _ = parts.shape
    total = parts[0]
    for z in range(1, far):
        total = total + parts[z]
    total = total * scale
    for d in range(out.shape[0]):
        out[d, :rows, :] = spec[...]
        out[d, rows:, :] = total


def grad_kernel(pairs, out_far, out, sems):
    _, n_ka, n_kl, chans, _ = out.shape
    half = chans // 2
    lanes = pairs.shape[2]
    copies = []
    part = n_kl // sems.shape[0]
    for kl in range(n_kl):
        s_re, s_im, d_re, d_im = (pairs[:, i * n_kl + kl, :] for i in range(4))
        s_h, s_l = split(jnp.concatenate([s_re, s_im], 0))
        a = jnp.concatenate([d_re, d_im], 0)
        b = jnp.concatenate([d_im, -d_re], 0)
        d_h, d_l = split(jnp.concatenate([a, b], 1))
        left = jnp.concatenate([s_h, s_l, s_h], 0)
        right = jnp.concatenate([d_h, d_h, d_l], 0)
        whole = dot_tn(left, right)
        for q in range(2):
            for ka in range(n_ka):
                for h in range(2):
                    r = h * lanes // 2 + ka * half
                    for g in range(2):
                        c = q * lanes + g * lanes // 2 + ka * half
                        out[q, ka, kl, h * half : (h + 1) * half, g * half : (g + 1) * half] = whole[r : r + half, c : c + half]
        if kl % part == part - 1:
            at = pl.ds(kl + 1 - part, part)
            copies.append(pltpu.make_async_copy(out.at[:, :, at], out_far.at[:, :, at], sems.at[kl // part]))
            copies[-1].start()
    for copy in copies:
        copy.wait()


def call(kernel, out_shape, *args, **more):
    return pl.pallas_call(
        kernel,
        out_shape=out_shape,
        compiler_params=pltpu.CompilerParams(vmem_limit_bytes=VMEM),
        **more,
    )(*args)


def shape(*dims, dtype=F32):
    return jax.ShapeDtypeStruct(dims, dtype)


def per_device(field, cotangent, spectral_weight, point_weight, bias):
    _, chans, cells_a, merged = field.shape
    cells_r = NR
    cells_l = merged // cells_r
    far, n_axial, n_dp = (lax.axis_size(name) for name in ("zh", "axial", "dp"))
    n_azim = far * NEAR
    _, _, loc_a, modes, _, _ = spectral_weight.shape
    tables = Tables(modes, chans, cells_a, cells_l, cells_r, n_azim, n_axial)
    total_cells = cells_a * n_azim * cells_l * n_axial * cells_r
    forward_scale = 1.0 / math.sqrt(total_cells)
    mode_scale = 1.0 / (modes * math.sqrt(modes))
    rows_x = chans * cells_a
    rows_k = 2 * modes * modes
    lanes = loc_a * chans
    block = (2 * modes, lanes)
    whole = (NEAR, n_axial, far, *block)
    held = [jnp.asarray(t) for t in (tables.halves, tables.turn, tables.place, tables.rows, tables.cols)]
    cells = jnp.asarray(tables.cells)
    x = field.reshape(rows_x, merged)
    cot = cotangent.reshape(rows_x, merged)
    near_axes = ("zl", "axial")

    def exchange(values, axes):
        flat = values.reshape(-1, *block)
        return lax.all_to_all(flat, axes, 0, 0, tiled=True).reshape(values.shape)

    def reduce(values):
        return exchange(call(sum_kernel, pltpu.VMEM((far, *block), F32), exchange(values, near_axes)), "zh")

    far_off = pl.BlockSpec(memory_space=pl.ANY)
    near_by = pl.BlockSpec(memory_space=pltpu.VMEM)

    def stay(array):
        return pltpu.with_memory_space_constraint(array, pltpu.HBM)

    field_shape = pltpu.VMEM((rows_x, merged), BF)
    x, cot, *held = map(stay, (x, cot, *held))
    held_shapes = [pltpu.VMEM(t.shape[2:] if i == 2 else t.shape, t.dtype) for i, t in enumerate(held)]
    first, *held = call(
        analysis_kernel,
        (pltpu.VMEM(whole, F32), *held_shapes, pltpu.VMEM((rows_x, rows_x), BF), pltpu.VMEM((rows_x, 128), F32)),
        x,
        *held,
        *map(stay, (cells, point_weight, bias[None])),
        in_specs=[far_off] * 9,
        out_specs=[near_by] * 8,
        scratch_shapes=[
            field_shape,
            pltpu.VMEM(cells.shape, BF),
            pltpu.VMEM(point_weight.shape, BF),
            pltpu.VMEM((1, chans), F32),
            pltpu.SemaphoreType.DMA((2,)),
            pltpu.SemaphoreType.DMA((9,)),
        ],
    )
    parts = reduce(first)

    def mix_body(*refs):
        mix_kernel(forward_scale, mode_scale, *refs)

    spec, mixed = call(
        mix_body,
        (shape(*block), shape(far, *block)),
        parts,
        spectral_weight[:, 0],
        scratch_shapes=[pltpu.VMEM((modes, lanes, 2 * lanes), BF)],
    )
    mixed = exchange(mixed, "zh")
    mixed = exchange(jnp.broadcast_to(mixed, whole), near_axes)
    group = (GROUPS, rows_x, merged // GROUPS)
    folded = (GROUPS, NEAR, rows_x, merged // GROUPS // NEAR)
    second = call(
        layer_kernel,
        pltpu.VMEM(whole, F32),
        mixed,
        *held,
        x,
        cot,
        in_specs=[near_by] * 8 + [far_off] * 2,
        out_specs=near_by,
        scratch_shapes=[
            pltpu.VMEM((rows_x, rows_k), F32),
            pltpu.VMEM(group, F32),
            pltpu.VMEM(folded, BF),
            pltpu.VMEM(folded, BF),
            field_shape,
            field_shape,
            pltpu.SemaphoreType.DMA((2,)),
        ],
    )
    parts = reduce(second)

    def join_body(*refs):
        join_kernel(mode_scale, *refs)

    pairs = call(join_body, shape(n_dp, 2 * block[0], lanes), parts, spec)
    pairs = lax.all_to_all(pairs, "dp", 0, 0, tiled=True)
    grad_dims = (2, loc_a, modes, chans, chans)
    grad = call(
        grad_kernel,
        pltpu.HBM(grad_dims, F32),
        pairs,
        in_specs=[near_by],
        out_specs=far_off,
        scratch_shapes=[pltpu.VMEM(grad_dims, F32), pltpu.SemaphoreType.DMA((4,))],
    )
    return grad[:, None]


def solution(mesh):
    n_dp, n_azim, n_axial = (mesh.shape[name] for name in ("dp", "azim", "axial"))
    fine = Mesh(mesh.devices.reshape(n_dp, n_azim // NEAR, NEAR, n_axial), ("dp", "zh", "zl", "axial"))
    azim = ("zh", "zl")
    in_specs = (
        P("dp", None, azim, "axial"),
        P("dp", None, azim, "axial"),
        P(None, azim, "axial", None, None, None),
        P(),
        P(),
    )
    out_specs = P(None, azim, "axial", None, None, None)
    return jax.shard_map(
        per_device, mesh=fine, in_specs=in_specs, out_specs=out_specs, check_vma=False
    )
```

```python
import math

import jax
import jax.numpy as jnp
import ml_dtypes
import numpy as np
from jax import lax
from jax.experimental import pallas as pl
from jax.experimental.pallas import tpu as pltpu
from jax.sharding import Mesh
from jax.sharding import PartitionSpec as P

NR = 64
NEAR = 2
BF = jnp.bfloat16
F32 = jnp.float32
GROUPS = 4
VMEM = 32 * 1024 * 1024


def split_table(values):
    high = values.astype(ml_dtypes.bfloat16)
    low = (values - high.astype(np.float64)).astype(ml_dtypes.bfloat16)
    return high, low


def split(values):
    high = values.astype(BF)
    return high, (values - high.astype(F32)).astype(BF)


def split3(values):
    high = values.astype(BF)
    rest = values - high.astype(F32)
    mid = rest.astype(BF)
    return high, mid, (rest - mid.astype(F32)).astype(BF)


def dot(a, b):
    return lax.dot_general(a, b, (((1,), (0,)), ((), ())), preferred_element_type=F32)


def dot_nt(a, b):
    return lax.dot_general(a, b, (((1,), (1,)), ((), ())), preferred_element_type=F32)


def dot_tn(a, b):
    return lax.dot_general(a, b, (((0,), (0,)), ((), ())), preferred_element_type=F32)


class Tables:
    def __init__(self, modes, chans, cells_a, cells_l, cells_r, n_azim, n_axial):
        total_a, total_l = cells_a * n_azim, cells_l * n_axial
        k = np.arange(modes)
        radial = np.outer(k, np.arange(cells_r)) % cells_r / cells_r
        radial = radial.reshape(modes // NEAR, NEAR, cells_r).transpose(1, 0, 2).reshape(modes, cells_r)
        group_l = cells_l // GROUPS
        axial = np.outer(k, np.arange(group_l)) % total_l / total_l
        angle = 2.0 * np.pi * (radial[:, None, None, :] + axial[None, :, :, None])
        angle = angle.reshape(modes * modes, group_l * cells_r)
        cells = np.stack(split_table(np.concatenate([np.cos(angle), -np.sin(angle)], 0)))
        order = np.arange(group_l).reshape(-1, 2, 2).transpose(0, 2, 1).reshape(-1)
        parted = cells.reshape(2, 2, NEAR, modes * modes // NEAR, group_l, 2, cells_r // 2)[..., order, 0, :]
        self.halves = parted.transpose(0, 2, 1, 3, 4, 5).reshape(2, NEAR, 2 * modes * modes // NEAR, group_l * cells_r // 2)
        angle = 2.0 * np.pi * (np.outer(np.arange(GROUPS) * group_l, k) % total_l / total_l)
        both = np.stack([np.cos(angle), np.sin(angle)], 1).astype(np.float32)
        self.rows = np.repeat(both[:, :, :, None], 128, 3)
        self.cols = np.tile(both, (1, 1, modes // NEAR))[:, :, None, :]
        half = chans // 2
        angle = 2.0 * np.pi * np.outer(np.arange(cells_a), k) / total_a
        same = np.eye(half)

        def spread(table):
            whole = table[None, :, :, None] * same[:, None, None, :]
            return whole.reshape(half * cells_a, modes * half)

        self.turn = np.stack(split_table(spread(np.cos(angle))) + split_table(spread(np.sin(angle))))
        loc_a = modes // n_axial
        axial = (np.outer(np.arange(n_axial) * cells_l, k) % total_l / total_l).reshape(1, n_axial, modes, 1)
        azim = (np.outer(np.arange(n_azim) * cells_a, k) % total_a / total_a).reshape(n_azim, n_axial, 1, loc_a, 1)
        azim = np.broadcast_to(azim, (n_azim, n_axial, 2, loc_a, half)).reshape(n_azim, 1, 1, modes * chans)
        angle = 2.0 * np.pi * (axial + azim)
        self.place = np.stack([np.cos(angle), np.sin(angle)], 2).astype(np.float32)


def azimuth_analysis(values, turn, place, out_ref):
    cos_h, cos_l, sin_h, sin_l = (turn[i] for i in range(4))
    rows, cols = values.shape[0] // 2, values.shape[1] // 2
    near, groups, far, block, lanes = out_ref.shape
    n_kl = block // 2
    reals, imags = [], []
    for h in range(2):
        high, low = split(values[:, h * cols : (h + 1) * cols])
        by_cos = dot(high, cos_h) + dot(low, cos_h) + dot(high, cos_l)
        by_sin = dot(high, sin_h) + dot(low, sin_h) + dot(high, sin_l)
        reals.append(by_cos[:rows] + by_sin[rows:])
        imags.append(by_cos[rows:] - by_sin[:rows])
    for g in range(groups):
        at = slice(g * lanes // 2, (g + 1) * lanes // 2)
        re = jnp.concatenate([r[:, at] for r in reals], 1).reshape(near, far, n_kl, lanes)
        im = jnp.concatenate([i[:, at] for i in imags], 1).reshape(near, far, n_kl, lanes)
        to = slice(g * lanes, (g + 1) * lanes)
        c, s = place[0, :, to], place[1, :, to]
        out_ref[:, g, :, :n_kl, :] = re * c + im * s
        out_ref[:, g, :, n_kl:, :] = im * c - re * s


def azimuth_synthesis(mixed, turn, place, synth):
    near, groups, far, block, lanes = mixed.shape
    n_kl = block // 2
    rows = near * far * n_kl
    reals, imags = [], []
    for g in range(groups):
        re, im = mixed[:, g, :, :n_kl, :], mixed[:, g, :, n_kl:, :]
        to = slice(g * lanes, (g + 1) * lanes)
        c, s = place[0, :, to], place[1, :, to]
        reals.append((re * c - im * s).reshape(rows, lanes))
        imags.append((im * c + re * s).reshape(rows, lanes))
    cos_h, cos_l, sin_h, sin_l = (turn[i] for i in range(4))

    def times(t_h, t_l, v):
        return dot_nt(t_h, v[0]) + dot_nt(t_h, v[1]) + dot_nt(t_l, v[0])

    half = synth.shape[0] // 2
    for h in range(2):
        at = slice(h * lanes // 2, (h + 1) * lanes // 2)
        re = split(jnp.concatenate([r[:, at] for r in reals], 1))
        im = split(jnp.concatenate([i[:, at] for i in imags], 1))
        real = times(cos_h, cos_l, re) - times(sin_h, sin_l, im)
        imag = times(sin_h, sin_l, re) + times(cos_h, cos_l, im)
        synth[h * half : (h + 1) * half, :rows] = real
        synth[h * half : (h + 1) * half, rows:] = imag


def add_group(total, part, group, rows):
    if group == 0:
        return part
    half, cols = part.shape[0] // 2, part.shape[1]
    n_kl = rows.shape[2]
    re, im = part[:half].reshape(-1, n_kl, cols), part[half:].reshape(-1, n_kl, cols)
    c, s = rows[group, 0][:, :1], rows[group, 1][:, :1]
    turned = jnp.concatenate([re * c + im * s, im * c - re * s], 0)
    return total + turned.reshape(part.shape)


def turn_group(values, group, cols):
    if group == 0:
        return split(values)
    half = values.shape[1] // 2
    re, im = values[:, :half], values[:, half:]
    c, s = cols[group, 0], cols[group, 1]
    return split(jnp.concatenate([re * c - im * s, im * c + re * s], 1))


def first_half():
    return lax.broadcasted_iota(jnp.int32, (1, 128), 1) % NR < NR // 2


def fold(values):
    a, b = values[:, :128], values[:, 128:]
    u = jnp.where(first_half(), a, pltpu.roll(b, NR // 2, 1))
    v = jnp.where(first_half(), pltpu.roll(a, 128 - NR // 2, 1), b)
    return u + v, u - v


def unfold(even, odd):
    u, v = even + odd, even - odd
    a = jnp.where(first_half(), u, pltpu.roll(v, NR // 2, 1))
    b = jnp.where(first_half(), pltpu.roll(u, 128 - NR // 2, 1), v)
    return a, b


def add_halves(totals, parts, group, halves, rows):
    out = []
    for p, (high, low) in enumerate(parts):
        both = dot_nt(halves[:, p].reshape(-1, halves.shape[3]), high)
        half = both.shape[0] // 2
        value = both[:half] + both[half:] + dot_nt(halves[0, p], low)
        out.append(add_group(totals[p], value, group, rows))
    return out


def join_halves(totals):
    part = totals[0].shape[0] // 2
    return jnp.concatenate([value[q * part : (q + 1) * part] for q in range(2) for value in totals], 0)


def start_columns(source, target, sems, widths):
    step = source.shape[1] // sum(widths)
    copies, at = [], 0
    for i, width in enumerate(widths):
        columns = pl.ds(at * step, width * step)
        copies.append(pltpu.make_async_copy(source.at[:, columns], target.at[:, columns], sems.at[i]))
        copies[-1].start()
        at += width
    return copies


def analysis_kernel(
    field, halves, turn, place, rows, cols, point_far, bias_far,
    out, halves_here, turn_here, place_here, rows_here, cols_here, out_mix, out_bias, x, point, bias, sems, more_sems,
):
    y = lax.axis_index("axial")
    z = lax.axis_index("zh") * NEAR + lax.axis_index("zl")
    pairs = (
        (point_far, point),
        (bias_far, bias),
        (halves, halves_here),
        (rows, rows_here),
        (turn, turn_here),
        (place.at[z, y], place_here),
        (cols, cols_here),
    )
    more = [pltpu.make_async_copy(a, b, more_sems.at[i]) for i, (a, b) in enumerate(pairs)]
    for copy in more[:4]:
        copy.start()
    first, rest = start_columns(field, x, sems, (1, GROUPS - 1))
    for copy in more[4:]:
        copy.start()
    step = x.shape[1] // GROUPS
    for copy in more[:2]:
        copy.wait()
    spread_rows(point, bias, out_mix, out_bias)
    for copy in (first, *more[2:4]):
        copy.wait()
    totals = [None] * NEAR
    for g in range(GROUPS):
        if g == 1:
            for copy in (rest, *more[4:]):
                copy.wait()
        values = x[:, g * step : (g + 1) * step].astype(F32)
        folded = zip(*(fold(values[:, j * 256 : (j + 1) * 256]) for j in range(step // 256)))
        parts = [split(jnp.concatenate(value, 1)) for value in folded]
        totals = add_halves(totals, parts, g, halves_here, rows_here)
    azimuth_analysis(join_halves(totals), turn_here, place_here, out)


def layer_kernel(
    mixed, halves, turn, place, rows, cols, mix, bias, field, cot_far, out, synth, pre, delta_h, delta_l, x, cot, sems
):
    copies = [pltpu.make_async_copy(field, x, sems.at[0]), pltpu.make_async_copy(cot_far, cot, sems.at[1])]
    for copy in copies:
        copy.start()
    azimuth_synthesis(mixed, turn, place, synth)
    step = x.shape[1] // GROUPS
    shift = jnp.concatenate([bias[...]] * (step // bias.shape[1]), 1)
    slope = math.sqrt(2.0 / math.pi)

    half = synth.shape[1] // 2
    part = half // NEAR

    def synthesize(g):
        sums = []
        for p in range(NEAR):
            at = [synth[:, q * half + p * part : q * half + (p + 1) * part] for q in range(2)]
            high, low = turn_group(jnp.concatenate(at, 1), g, cols)
            sums.append(dot(high, halves[0, p]) + dot(low, halves[0, p]) + dot(high, halves[1, p]))
        for j in range(step // 256):
            a, b = unfold(*(value[:, j * 128 : (j + 1) * 128] for value in sums))
            pre[g, :, j * 256 : j * 256 + 128] = a
            pre[g, :, j * 256 + 128 : (j + 1) * 256] = b

    def activate(g):
        at = slice(g * step, (g + 1) * step)
        value = pre[g] + dot(mix[...], x[:, at]) + shift
        square = value * value
        t = jnp.tanh(value * (slope + (slope * 0.044715) * square))
        inner = value * (slope + (3.0 * slope * 0.044715) * square)
        share = 0.5 + 0.5 * t
        delta = cot[:, at].astype(F32) * (share + share * (inner - inner * t))
        for j in range(step // 256):
            to = slice(j * 128, (j + 1) * 128)
            for p, value in enumerate(fold(delta[:, j * 256 : (j + 1) * 256])):
                delta_h[g, p, :, to], delta_l[g, p, :, to] = split(value)

    def analyze(g, totals):
        parts = [(delta_h[g, p], delta_l[g, p]) for p in range(NEAR)]
        return add_halves(totals, parts, g, halves, rows)

    ahead = 2
    for g in range(ahead):
        synthesize(g)
    for copy in copies:
        copy.wait()
    totals = [None] * NEAR
    for g in range(GROUPS):
        if ahead <= g + 1 < GROUPS:
            synthesize(g + 1)
        activate(g)
        if g > 0:
            totals = analyze(g - 1, totals)
    totals = analyze(GROUPS - 1, totals)
    azimuth_analysis(join_halves(totals), turn, place, out)


def spread_rows(point, bias, out_mix, out_bias):
    chans, rows = point.shape[0], out_mix.shape[0]
    cells = rows // chans

    def owner(shape, axis):
        i, c = lax.broadcasted_iota(jnp.int32, shape, axis), lax.broadcasted_iota(jnp.int32, shape, 1 - axis)
        return (i >= c * cells) & (i < (c + 1) * cells)

    left = owner((rows, chans), 0)
    right = jnp.where(owner((chans, rows), 1), 1.0, 0.0).astype(BF)
    wide = dot(dot(jnp.where(left, 1.0, 0.0).astype(BF), point[...]).astype(BF), right)
    i = lax.broadcasted_iota(jnp.int32, (rows, rows), 0)
    j = lax.broadcasted_iota(jnp.int32, (rows, rows), 1)
    out_mix[...] = jnp.where(i % cells == j % cells, wide, 0.0).astype(BF)
    column = jnp.sum(jnp.where(left, bias[...], 0.0), 1, keepdims=True)
    out_bias[...] = jnp.broadcast_to(column, out_bias.shape)


def pack_weights(weight, out):
    n_q, n_ka, n_kl, chans, _ = weight.shape
    half = chans // 2
    lanes = n_ka * chans
    o = lax.broadcasted_iota(jnp.int32, (chans, lanes), 0)
    lane = lax.broadcasted_iota(jnp.int32, (chans, lanes), 1)
    for ka in range(n_ka):
        to = jnp.where(o < half, o, o + (n_ka - 1) * half) + ka * half
        place = jnp.where(lane == to, 1.0, 0.0).astype(BF)
        for q in range(n_q):
            moved = dot(weight[q, ka].reshape(n_kl * chans, chans), place).astype(BF)
            moved = moved.reshape(n_kl, 2, half, lanes)
            for h in range(2):
                at = h * lanes // 2 + ka * half
                out[:, at : at + half, q * lanes : (q + 1) * lanes] = moved[:, h]


def sum_kernel(parts, out):
    near, groups, *_ = parts.shape
    total = None
    for place in range(near * groups):
        part = parts[place // groups, place % groups]
        total = part if total is None else total + part
    out[...] = total


def mix_kernel(scale, out_scale, parts, raw, spec, out, weight):
    pack_weights(raw, weight)
    far, rows, lanes = parts.shape
    n_kl = rows // 2
    total = parts[0]
    for z in range(1, far):
        total = total + parts[z]
    total = total * scale
    spec[...] = total
    stack = jnp.concatenate([*split3(total[:n_kl]), *split3(total[n_kl:])], 0)
    row = lax.broadcasted_iota(jnp.int32, (stack.shape[0], 2 * lanes), 0) % n_kl
    got = jnp.zeros((stack.shape[0], 2 * lanes), F32)
    for kl in range(n_kl):
        got = jnp.where(row == kl, dot(stack, weight[kl]), got)
    by_re = got[:n_kl] + got[n_kl : 2 * n_kl] + got[2 * n_kl : 3 * n_kl]
    by_im = got[3 * n_kl : 4 * n_kl] + got[4 * n_kl : 5 * n_kl] + got[5 * n_kl :]
    re = (by_re[:, :lanes] - by_im[:, lanes:]) * out_scale
    im = (by_re[:, lanes:] + by_im[:, :lanes]) * out_scale
    for z in range(far):
        out[z, :n_kl, :] = re
        out[z, n_kl:, :] = im


def join_kernel(scale, parts, spec, out):
    far, rows, _ = parts.shape
    total = parts[0]
    for z in range(1, far):
        total = total + parts[z]
    total = total * scale
    for d in range(out.shape[0]):
        out[d, :rows, :] = spec[...]
        out[d, rows:, :] = total


def grad_kernel(pairs, out_far, out, sems):
    _, n_ka, n_kl, chans, _ = out.shape
    half = chans // 2
    lanes = pairs.shape[2]
    copies = []
    part = n_kl // sems.shape[0]
    for kl in range(n_kl):
        s_re, s_im, d_re, d_im = (pairs[:, i * n_kl + kl, :] for i in range(4))
        s_h, s_l = split(jnp.concatenate([s_re, s_im], 0))
        a = jnp.concatenate([d_re, d_im], 0)
        b = jnp.concatenate([d_im, -d_re], 0)
        d_h, d_l = split(jnp.concatenate([a, b], 1))
        left = jnp.concatenate([s_h, s_l, s_h], 0)
        right = jnp.concatenate([d_h, d_h, d_l], 0)
        whole = dot_tn(left, right)
        for q in range(2):
            for ka in range(n_ka):
                for h in range(2):
                    r = h * lanes // 2 + ka * half
                    for g in range(2):
                        c = q * lanes + g * lanes // 2 + ka * half
                        out[q, ka, kl, h * half : (h + 1) * half, g * half : (g + 1) * half] = whole[r : r + half, c : c + half]
        if kl % part == part - 1:
            at = pl.ds(kl + 1 - part, part)
            copies.append(pltpu.make_async_copy(out.at[:, :, at], out_far.at[:, :, at], sems.at[kl // part]))
            copies[-1].start()
    for copy in copies:
        copy.wait()


def call(kernel, out_shape, *args, **more):
    return pl.pallas_call(
        kernel,
        out_shape=out_shape,
        compiler_params=pltpu.CompilerParams(vmem_limit_bytes=VMEM),
        **more,
    )(*args)


def shape(*dims, dtype=F32):
    return jax.ShapeDtypeStruct(dims, dtype)


def per_device(field, cotangent, spectral_weight, point_weight, bias):
    _, chans, cells_a, merged = field.shape
    cells_r = NR
    cells_l = merged // cells_r
    far, n_axial, n_dp = (lax.axis_size(name) for name in ("zh", "axial", "dp"))
    n_azim = far * NEAR
    _, _, loc_a, modes, _, _ = spectral_weight.shape
    tables = Tables(modes, chans, cells_a, cells_l, cells_r, n_azim, n_axial)
    total_cells = cells_a * n_azim * cells_l * n_axial * cells_r
    forward_scale = 1.0 / math.sqrt(total_cells)
    mode_scale = 1.0 / (modes * math.sqrt(modes))
    rows_x = chans * cells_a
    rows_k = 2 * modes * modes
    lanes = loc_a * chans
    block = (2 * modes, lanes)
    whole = (NEAR, n_axial, far, *block)
    held = [jnp.asarray(t) for t in (tables.halves, tables.turn, tables.place, tables.rows, tables.cols)]
    x = field.reshape(rows_x, merged)
    cot = cotangent.reshape(rows_x, merged)
    near_axes = ("zl", "axial")

    def exchange(values, axes):
        flat = values.reshape(-1, *block)
        return lax.all_to_all(flat, axes, 0, 0, tiled=True).reshape(values.shape)

    def reduce(values):
        return exchange(call(sum_kernel, pltpu.VMEM((far, *block), F32), exchange(values, near_axes)), "zh")

    far_off = pl.BlockSpec(memory_space=pl.ANY)
    near_by = pl.BlockSpec(memory_space=pltpu.VMEM)

    def stay(array):
        return pltpu.with_memory_space_constraint(array, pltpu.HBM)

    field_shape = pltpu.VMEM((rows_x, merged), BF)
    x, cot, *held = map(stay, (x, cot, *held))
    held_shapes = [pltpu.VMEM(t.shape[2:] if i == 2 else t.shape, t.dtype) for i, t in enumerate(held)]
    first, *held = call(
        analysis_kernel,
        (pltpu.VMEM(whole, F32), *held_shapes, pltpu.VMEM((rows_x, rows_x), BF), pltpu.VMEM((rows_x, 128), F32)),
        x,
        *held,
        *map(stay, (point_weight, bias[None])),
        in_specs=[far_off] * 8,
        out_specs=[near_by] * 8,
        scratch_shapes=[
            field_shape,
            pltpu.VMEM(point_weight.shape, BF),
            pltpu.VMEM((1, chans), F32),
            pltpu.SemaphoreType.DMA((2,)),
            pltpu.SemaphoreType.DMA((7,)),
        ],
    )
    parts = reduce(first)

    def mix_body(*refs):
        mix_kernel(forward_scale, mode_scale, *refs)

    spec, mixed = call(
        mix_body,
        (shape(*block), shape(far, *block)),
        parts,
        spectral_weight[:, 0],
        scratch_shapes=[pltpu.VMEM((modes, lanes, 2 * lanes), BF)],
    )
    mixed = exchange(mixed, "zh")
    mixed = exchange(jnp.broadcast_to(mixed, whole), near_axes)
    group = (GROUPS, rows_x, merged // GROUPS)
    folded = (GROUPS, NEAR, rows_x, merged // GROUPS // NEAR)
    second = call(
        layer_kernel,
        pltpu.VMEM(whole, F32),
        mixed,
        *held,
        x,
        cot,
        in_specs=[near_by] * 8 + [far_off] * 2,
        out_specs=near_by,
        scratch_shapes=[
            pltpu.VMEM((rows_x, rows_k), F32),
            pltpu.VMEM(group, F32),
            pltpu.VMEM(folded, BF),
            pltpu.VMEM(folded, BF),
            field_shape,
            field_shape,
            pltpu.SemaphoreType.DMA((2,)),
        ],
    )
    parts = reduce(second)

    def join_body(*refs):
        join_kernel(mode_scale, *refs)

    pairs = call(join_body, shape(n_dp, 2 * block[0], lanes), parts, spec)
    pairs = lax.all_to_all(pairs, "dp", 0, 0, tiled=True)
    grad_dims = (2, loc_a, modes, chans, chans)
    grad = call(
        grad_kernel,
        pltpu.HBM(grad_dims, F32),
        pairs,
        in_specs=[near_by],
        out_specs=far_off,
        scratch_shapes=[pltpu.VMEM(grad_dims, F32), pltpu.SemaphoreType.DMA((4,))],
    )
    return grad[:, None]


def solution(mesh):
    n_dp, n_azim, n_axial = (mesh.shape[name] for name in ("dp", "azim", "axial"))
    fine = Mesh(mesh.devices.reshape(n_dp, n_azim // NEAR, NEAR, n_axial), ("dp", "zh", "zl", "axial"))
    azim = ("zh", "zl")
    in_specs = (
        P("dp", None, azim, "axial"),
        P("dp", None, azim, "axial"),
        P(None, azim, "axial", None, None, None),
        P(),
        P(),
    )
    out_specs = P(None, azim, "axial", None, None, None)
    return jax.shard_map(
        per_device, mesh=fine, in_specs=in_specs, out_specs=out_specs, check_vma=False
    )
```

```python
import math

import jax
import jax.numpy as jnp
import ml_dtypes
import numpy as np
from jax import lax
from jax.experimental import pallas as pl
from jax.experimental.pallas import tpu as pltpu
from jax.sharding import Mesh
from jax.sharding import PartitionSpec as P

NR = 64
NEAR = 2
BF = jnp.bfloat16
F32 = jnp.float32
GROUPS = 4
VMEM = 32 * 1024 * 1024


def split_table(values):
    high = values.astype(ml_dtypes.bfloat16)
    low = (values - high.astype(np.float64)).astype(ml_dtypes.bfloat16)
    return high, low


def split(values):
    high = values.astype(BF)
    return high, (values - high.astype(F32)).astype(BF)


def dot(a, b):
    return lax.dot_general(a, b, (((1,), (0,)), ((), ())), preferred_element_type=F32)


def dot_nt(a, b):
    return lax.dot_general(a, b, (((1,), (1,)), ((), ())), preferred_element_type=F32)


def dot_tn(a, b):
    return lax.dot_general(a, b, (((0,), (0,)), ((), ())), preferred_element_type=F32)


class Tables:
    def __init__(self, modes, chans, cells_a, cells_l, cells_r, n_azim, n_axial):
        total_a, total_l = cells_a * n_azim, cells_l * n_axial
        k = np.arange(modes)
        radial = np.outer(k, np.arange(cells_r)) % cells_r / cells_r
        radial = radial.reshape(modes // NEAR, NEAR, cells_r).transpose(1, 0, 2).reshape(modes, cells_r)
        group_l = cells_l // GROUPS
        axial = np.outer(k, np.arange(group_l)) % total_l / total_l
        angle = 2.0 * np.pi * (radial[:, None, None, :] + axial[None, :, :, None])
        angle = angle.reshape(modes * modes, group_l * cells_r)
        cells = np.stack(split_table(np.concatenate([np.cos(angle), -np.sin(angle)], 0)))
        order = np.arange(group_l).reshape(-1, 2, 2).transpose(0, 2, 1).reshape(-1)
        parted = cells.reshape(2, 2, NEAR, modes * modes // NEAR, group_l, 2, cells_r // 2)[..., order, 0, :]
        self.halves = parted.transpose(0, 2, 1, 3, 4, 5).reshape(2, NEAR, 2 * modes * modes // NEAR, group_l * cells_r // 2)
        angle = 2.0 * np.pi * (np.outer(np.arange(GROUPS) * group_l, k) % total_l / total_l)
        both = np.stack([np.cos(angle), np.sin(angle)], 1).astype(np.float32)
        self.rows = np.repeat(both[:, :, :, None], 128, 3)
        self.cols = np.tile(both, (1, 1, modes // NEAR))[:, :, None, :]
        half = chans // 2
        angle = 2.0 * np.pi * np.outer(np.arange(cells_a), k) / total_a
        same = np.eye(half)

        def spread(table):
            whole = table[None, :, :, None] * same[:, None, None, :]
            return whole.reshape(half * cells_a, modes * half)

        self.turn = np.stack(split_table(spread(np.cos(angle))) + split_table(spread(np.sin(angle))))
        loc_a = modes // n_axial
        axial = (np.outer(np.arange(n_axial) * cells_l, k) % total_l / total_l).reshape(1, n_axial, modes, 1)
        azim = (np.outer(np.arange(n_azim) * cells_a, k) % total_a / total_a).reshape(n_azim, n_axial, 1, loc_a, 1)
        azim = np.broadcast_to(azim, (n_azim, n_axial, 2, loc_a, half)).reshape(n_azim, 1, 1, modes * chans)
        angle = 2.0 * np.pi * (axial + azim)
        self.place = np.stack([np.cos(angle), np.sin(angle)], 2).astype(np.float32)


def azimuth_analysis(values, turn, place, out_ref):
    cos_h, cos_l, sin_h, sin_l = (turn[i] for i in range(4))
    rows, cols = values.shape[0] // 2, values.shape[1] // 2
    near, groups, far, block, lanes = out_ref.shape
    n_kl = block // 2
    reals, imags = [], []
    for h in range(2):
        high, low = split(values[:, h * cols : (h + 1) * cols])
        by_cos = dot(high, cos_h) + dot(low, cos_h) + dot(high, cos_l)
        by_sin = dot(high, sin_h) + dot(low, sin_h) + dot(high, sin_l)
        reals.append(by_cos[:rows] + by_sin[rows:])
        imags.append(by_cos[rows:] - by_sin[:rows])
    for g in range(groups):
        at = slice(g * lanes // 2, (g + 1) * lanes // 2)
        re = jnp.concatenate([r[:, at] for r in reals], 1).reshape(near, far, n_kl, lanes)
        im = jnp.concatenate([i[:, at] for i in imags], 1).reshape(near, far, n_kl, lanes)
        to = slice(g * lanes, (g + 1) * lanes)
        c, s = place[0, :, to], place[1, :, to]
        out_ref[:, g, :, :n_kl, :] = re * c + im * s
        out_ref[:, g, :, n_kl:, :] = im * c - re * s


def azimuth_synthesis(mixed, turn, place, synth):
    near, groups, far, block, lanes = mixed.shape
    n_kl = block // 2
    rows = near * far * n_kl
    reals, imags = [], []
    for g in range(groups):
        re, im = mixed[:, g, :, :n_kl, :], mixed[:, g, :, n_kl:, :]
        to = slice(g * lanes, (g + 1) * lanes)
        c, s = place[0, :, to], place[1, :, to]
        reals.append((re * c - im * s).reshape(rows, lanes))
        imags.append((im * c + re * s).reshape(rows, lanes))
    cos_h, cos_l, sin_h, sin_l = (turn[i] for i in range(4))

    def times(t_h, t_l, v):
        return dot_nt(t_h, v[0]) + dot_nt(t_h, v[1]) + dot_nt(t_l, v[0])

    half = synth.shape[0] // 2
    for h in range(2):
        at = slice(h * lanes // 2, (h + 1) * lanes // 2)
        re = split(jnp.concatenate([r[:, at] for r in reals], 1))
        im = split(jnp.concatenate([i[:, at] for i in imags], 1))
        real = times(cos_h, cos_l, re) - times(sin_h, sin_l, im)
        imag = times(sin_h, sin_l, re) + times(cos_h, cos_l, im)
        synth[h * half : (h + 1) * half, :rows] = real
        synth[h * half : (h + 1) * half, rows:] = imag


def add_group(total, part, group, rows):
    if group == 0:
        return part
    half, cols = part.shape[0] // 2, part.shape[1]
    n_kl = rows.shape[2]
    re, im = part[:half].reshape(-1, n_kl, cols), part[half:].reshape(-1, n_kl, cols)
    c, s = rows[group, 0][:, :1], rows[group, 1][:, :1]
    turned = jnp.concatenate([re * c + im * s, im * c - re * s], 0)
    return total + turned.reshape(part.shape)


def turn_group(values, group, cols):
    if group == 0:
        return split(values)
    half = values.shape[1] // 2
    re, im = values[:, :half], values[:, half:]
    c, s = cols[group, 0], cols[group, 1]
    return split(jnp.concatenate([re * c - im * s, im * c + re * s], 1))


def first_half():
    return lax.broadcasted_iota(jnp.int32, (1, 128), 1) % NR < NR // 2


def fold(values):
    a, b = values[:, :128], values[:, 128:]
    u = jnp.where(first_half(), a, pltpu.roll(b, NR // 2, 1))
    v = jnp.where(first_half(), pltpu.roll(a, 128 - NR // 2, 1), b)
    return u + v, u - v


def unfold(even, odd):
    u, v = even + odd, even - odd
    a = jnp.where(first_half(), u, pltpu.roll(v, NR // 2, 1))
    b = jnp.where(first_half(), pltpu.roll(u, 128 - NR // 2, 1), v)
    return a, b


def add_halves(totals, parts, group, halves, rows):
    out = []
    for p, (high, low) in enumerate(parts):
        both = dot_nt(halves[:, p].reshape(-1, halves.shape[3]), high)
        half = both.shape[0] // 2
        value = both[:half] + both[half:] + dot_nt(halves[0, p], low)
        out.append(add_group(totals[p], value, group, rows))
    return out


def join_halves(totals):
    part = totals[0].shape[0] // 2
    return jnp.concatenate([value[q * part : (q + 1) * part] for q in range(2) for value in totals], 0)


def start_columns(source, target, sems, widths):
    step = source.shape[1] // sum(widths)
    copies, at = [], 0
    for i, width in enumerate(widths):
        columns = pl.ds(at * step, width * step)
        copies.append(pltpu.make_async_copy(source.at[:, columns], target.at[:, columns], sems.at[i]))
        copies[-1].start()
        at += width
    return copies


def analysis_kernel(
    field, halves, turn, place, rows, cols, point_far, bias_far,
    out, halves_here, turn_here, place_here, rows_here, cols_here, out_mix, out_bias, x, point, bias, sems, more_sems,
):
    y = lax.axis_index("axial")
    z = lax.axis_index("zh") * NEAR + lax.axis_index("zl")
    pairs = (
        (point_far, point),
        (bias_far, bias),
        (halves, halves_here),
        (rows, rows_here),
        (turn, turn_here),
        (place.at[z, y], place_here),
        (cols, cols_here),
    )
    more = [pltpu.make_async_copy(a, b, more_sems.at[i]) for i, (a, b) in enumerate(pairs)]
    for copy in more[:4]:
        copy.start()
    first, rest = start_columns(field, x, sems, (1, GROUPS - 1))
    for copy in more[4:]:
        copy.start()
    step = x.shape[1] // GROUPS
    for copy in more[:2]:
        copy.wait()
    spread_rows(point, bias, out_mix, out_bias)
    for copy in (first, *more[2:4]):
        copy.wait()
    totals = [None] * NEAR
    for g in range(GROUPS):
        if g == 1:
            for copy in (rest, *more[4:]):
                copy.wait()
        values = x[:, g * step : (g + 1) * step].astype(F32)
        folded = zip(*(fold(values[:, j * 256 : (j + 1) * 256]) for j in range(step // 256)))
        parts = [split(jnp.concatenate(value, 1)) for value in folded]
        totals = add_halves(totals, parts, g, halves_here, rows_here)
    azimuth_analysis(join_halves(totals), turn_here, place_here, out)


def layer_kernel(
    mixed, halves, turn, place, rows, cols, mix, bias, field, cot_far, out, synth, pre, delta_h, delta_l, x, cot, sems
):
    copies = [pltpu.make_async_copy(field, x, sems.at[0]), pltpu.make_async_copy(cot_far, cot, sems.at[1])]
    for copy in copies:
        copy.start()
    azimuth_synthesis(mixed, turn, place, synth)
    step = x.shape[1] // GROUPS
    lane = lax.broadcasted_iota(jnp.int32, (1, bias.shape[1]), 1)
    synth[:, : bias.shape[1]] += jnp.where(lane == 0, bias[...], 0.0)
    slope = math.sqrt(2.0 / math.pi)

    half = synth.shape[1] // 2
    part = half // NEAR

    def synthesize(g):
        sums = []
        for p in range(NEAR):
            at = [synth[:, q * half + p * part : q * half + (p + 1) * part] for q in range(2)]
            high, low = turn_group(jnp.concatenate(at, 1), g, cols)
            sums.append(dot(high, halves[0, p]) + dot(low, halves[0, p]) + dot(high, halves[1, p]))
        for j in range(step // 256):
            a, b = unfold(*(value[:, j * 128 : (j + 1) * 128] for value in sums))
            pre[g, :, j * 256 : j * 256 + 128] = a
            pre[g, :, j * 256 + 128 : (j + 1) * 256] = b

    def activate(g):
        at = slice(g * step, (g + 1) * step)
        value = pre[g] + dot(mix[...], x[:, at])
        square = value * value
        t = jnp.tanh(value * (slope + (slope * 0.044715) * square))
        inner = value * (slope + (3.0 * slope * 0.044715) * square)
        share = 0.5 + 0.5 * t
        delta = cot[:, at].astype(F32) * (share + share * (inner - inner * t))
        for j in range(step // 256):
            to = slice(j * 128, (j + 1) * 128)
            for p, value in enumerate(fold(delta[:, j * 256 : (j + 1) * 256])):
                delta_h[g, p, :, to], delta_l[g, p, :, to] = split(value)

    def analyze(g, totals):
        parts = [(delta_h[g, p], delta_l[g, p]) for p in range(NEAR)]
        return add_halves(totals, parts, g, halves, rows)

    ahead = 2
    for g in range(ahead):
        synthesize(g)
    for copy in copies:
        copy.wait()
    totals = [None] * NEAR
    for g in range(GROUPS):
        if ahead <= g + 1 < GROUPS:
            synthesize(g + 1)
        activate(g)
        if g > 0:
            totals = analyze(g - 1, totals)
    totals = analyze(GROUPS - 1, totals)
    azimuth_analysis(join_halves(totals), turn, place, out)


def spread_rows(point, bias, out_mix, out_bias):
    chans, rows = point.shape[0], out_mix.shape[0]
    cells = rows // chans

    def owner(shape, axis):
        i, c = lax.broadcasted_iota(jnp.int32, shape, axis), lax.broadcasted_iota(jnp.int32, shape, 1 - axis)
        return (i >= c * cells) & (i < (c + 1) * cells)

    left = owner((rows, chans), 0)
    right = jnp.where(owner((chans, rows), 1), 1.0, 0.0).astype(BF)
    wide = dot(dot(jnp.where(left, 1.0, 0.0).astype(BF), point[...]).astype(BF), right)
    i = lax.broadcasted_iota(jnp.int32, (rows, rows), 0)
    j = lax.broadcasted_iota(jnp.int32, (rows, rows), 1)
    out_mix[...] = jnp.where(i % cells == j % cells, wide, 0.0).astype(BF)
    column = jnp.sum(jnp.where(left, bias[...], 0.0), 1, keepdims=True)
    out_bias[...] = jnp.broadcast_to(column, out_bias.shape)


def pack_weights(weight, out):
    n_q, n_ka, n_kl, chans, _ = weight.shape
    half = chans // 2
    lanes = n_ka * chans
    o = lax.broadcasted_iota(jnp.int32, (chans, lanes), 0)
    lane = lax.broadcasted_iota(jnp.int32, (chans, lanes), 1)
    for ka in range(n_ka):
        to = jnp.where(o < half, o, o + (n_ka - 1) * half) + ka * half
        place = jnp.where(lane == to, 1.0, 0.0).astype(BF)
        for q in range(n_q):
            moved = dot(weight[q, ka].reshape(n_kl * chans, chans), place).astype(BF)
            moved = moved.reshape(n_kl, 2, half, lanes)
            for h in range(2):
                at = h * lanes // 2 + ka * half
                out[:, at : at + half, q * lanes : (q + 1) * lanes] = moved[:, h]


def sum_kernel(parts, out):
    near, groups, *_ = parts.shape
    total = None
    for place in range(near * groups):
        part = parts[place // groups, place % groups]
        total = part if total is None else total + part
    out[...] = total


def mix_kernel(scale, out_scale, parts, raw, spec, out, weight):
    pack_weights(raw, weight)
    far, rows, lanes = parts.shape
    n_kl = rows // 2
    total = parts[0]
    for z in range(1, far):
        total = total + parts[z]
    total = total * scale
    spec[...] = total
    stack = jnp.concatenate([*split(total[:n_kl]), *split(total[n_kl:])], 0)
    row = lax.broadcasted_iota(jnp.int32, (stack.shape[0], 2 * lanes), 0) % n_kl
    got = jnp.zeros((stack.shape[0], 2 * lanes), F32)
    for kl in range(n_kl):
        got = jnp.where(row == kl, dot(stack, weight[kl]), got)
    by_re = got[:n_kl] + got[n_kl : 2 * n_kl]
    by_im = got[2 * n_kl : 3 * n_kl] + got[3 * n_kl :]
    re = (by_re[:, :lanes] - by_im[:, lanes:]) * out_scale
    im = (by_re[:, lanes:] + by_im[:, :lanes]) * out_scale
    for z in range(far):
        out[z, :n_kl, :] = re
        out[z, n_kl:, :] = im


def join_kernel(scale, parts, spec, out):
    far, rows, _ = parts.shape
    total = parts[0]
    for z in range(1, far):
        total = total + parts[z]
    total = total * scale
    for d in range(out.shape[0]):
        out[d, :rows, :] = spec[...]
        out[d, rows:, :] = total


def grad_kernel(pairs, out_far, out, sems):
    _, n_ka, n_kl, chans, _ = out.shape
    half = chans // 2
    lanes = pairs.shape[2]
    copies = []
    part = n_kl // sems.shape[0]
    for kl in range(n_kl):
        s_re, s_im, d_re, d_im = (pairs[:, i * n_kl + kl, :] for i in range(4))
        s_h, s_l = split(jnp.concatenate([s_re, s_im], 0))
        a = jnp.concatenate([d_re, d_im], 0)
        b = jnp.concatenate([d_im, -d_re], 0)
        d_h, d_l = split(jnp.concatenate([a, b], 1))
        left = jnp.concatenate([s_h, s_l, s_h], 0)
        right = jnp.concatenate([d_h, d_h, d_l], 0)
        whole = dot_tn(left, right)
        for q in range(2):
            for ka in range(n_ka):
                for h in range(2):
                    r = h * lanes // 2 + ka * half
                    for g in range(2):
                        c = q * lanes + g * lanes // 2 + ka * half
                        out[q, ka, kl, h * half : (h + 1) * half, g * half : (g + 1) * half] = whole[r : r + half, c : c + half]
        if kl % part == part - 1:
            at = pl.ds(kl + 1 - part, part)
            copies.append(pltpu.make_async_copy(out.at[:, :, at], out_far.at[:, :, at], sems.at[kl // part]))
            copies[-1].start()
    for copy in copies:
        copy.wait()


def call(kernel, out_shape, *args, **more):
    return pl.pallas_call(
        kernel,
        out_shape=out_shape,
        compiler_params=pltpu.CompilerParams(vmem_limit_bytes=VMEM),
        **more,
    )(*args)


def shape(*dims, dtype=F32):
    return jax.ShapeDtypeStruct(dims, dtype)


def per_device(field, cotangent, spectral_weight, point_weight, bias):
    _, chans, cells_a, merged = field.shape
    cells_r = NR
    cells_l = merged // cells_r
    far, n_axial, n_dp = (lax.axis_size(name) for name in ("zh", "axial", "dp"))
    n_azim = far * NEAR
    _, _, loc_a, modes, _, _ = spectral_weight.shape
    tables = Tables(modes, chans, cells_a, cells_l, cells_r, n_azim, n_axial)
    total_cells = cells_a * n_azim * cells_l * n_axial * cells_r
    forward_scale = 1.0 / math.sqrt(total_cells)
    mode_scale = 1.0 / (modes * math.sqrt(modes))
    rows_x = chans * cells_a
    rows_k = 2 * modes * modes
    lanes = loc_a * chans
    block = (2 * modes, lanes)
    whole = (NEAR, n_axial, far, *block)
    held = [jnp.asarray(t) for t in (tables.halves, tables.turn, tables.place, tables.rows, tables.cols)]
    x = field.reshape(rows_x, merged)
    cot = cotangent.reshape(rows_x, merged)
    near_axes = ("zl", "axial")

    def exchange(values, axes):
        flat = values.reshape(-1, *block)
        return lax.all_to_all(flat, axes, 0, 0, tiled=True).reshape(values.shape)

    def reduce(values):
        return exchange(call(sum_kernel, pltpu.VMEM((far, *block), F32), exchange(values, near_axes)), "zh")

    far_off = pl.BlockSpec(memory_space=pl.ANY)
    near_by = pl.BlockSpec(memory_space=pltpu.VMEM)

    def stay(array):
        return pltpu.with_memory_space_constraint(array, pltpu.HBM)

    field_shape = pltpu.VMEM((rows_x, merged), BF)
    x, cot, *held = map(stay, (x, cot, *held))
    held_shapes = [pltpu.VMEM(t.shape[2:] if i == 2 else t.shape, t.dtype) for i, t in enumerate(held)]
    first, *held = call(
        analysis_kernel,
        (pltpu.VMEM(whole, F32), *held_shapes, pltpu.VMEM((rows_x, rows_x), BF), pltpu.VMEM((rows_x, 128), F32)),
        x,
        *held,
        *map(stay, (point_weight, bias[None])),
        in_specs=[far_off] * 8,
        out_specs=[near_by] * 8,
        scratch_shapes=[
            field_shape,
            pltpu.VMEM(point_weight.shape, BF),
            pltpu.VMEM((1, chans), F32),
            pltpu.SemaphoreType.DMA((2,)),
            pltpu.SemaphoreType.DMA((7,)),
        ],
    )
    parts = reduce(first)

    def mix_body(*refs):
        mix_kernel(forward_scale, mode_scale, *refs)

    spec, mixed = call(
        mix_body,
        (shape(*block), shape(far, *block)),
        parts,
        spectral_weight[:, 0],
        scratch_shapes=[pltpu.VMEM((modes, lanes, 2 * lanes), BF)],
    )
    mixed = exchange(mixed, "zh")
    mixed = exchange(jnp.broadcast_to(mixed, whole), near_axes)
    group = (GROUPS, rows_x, merged // GROUPS)
    folded = (GROUPS, NEAR, rows_x, merged // GROUPS // NEAR)
    second = call(
        layer_kernel,
        pltpu.VMEM(whole, F32),
        mixed,
        *held,
        x,
        cot,
        in_specs=[near_by] * 8 + [far_off] * 2,
        out_specs=near_by,
        scratch_shapes=[
            pltpu.VMEM((rows_x, rows_k), F32),
            pltpu.VMEM(group, F32),
            pltpu.VMEM(folded, BF),
            pltpu.VMEM(folded, BF),
            field_shape,
            field_shape,
            pltpu.SemaphoreType.DMA((2,)),
        ],
    )
    parts = reduce(second)

    def join_body(*refs):
        join_kernel(mode_scale, *refs)

    pairs = call(join_body, shape(n_dp, 2 * block[0], lanes), parts, spec)
    pairs = lax.all_to_all(pairs, "dp", 0, 0, tiled=True)
    grad_dims = (2, loc_a, modes, chans, chans)
    grad = call(
        grad_kernel,
        pltpu.HBM(grad_dims, F32),
        pairs,
        in_specs=[near_by],
        out_specs=far_off,
        scratch_shapes=[pltpu.VMEM(grad_dims, F32), pltpu.SemaphoreType.DMA((8,))],
    )
    return grad[:, None]


def solution(mesh):
    n_dp, n_azim, n_axial = (mesh.shape[name] for name in ("dp", "azim", "axial"))
    fine = Mesh(mesh.devices.reshape(n_dp, n_azim // NEAR, NEAR, n_axial), ("dp", "zh", "zl", "axial"))
    azim = ("zh", "zl")
    in_specs = (
        P("dp", None, azim, "axial"),
        P("dp", None, azim, "axial"),
        P(None, azim, "axial", None, None, None),
        P(),
        P(),
    )
    out_specs = P(None, azim, "axial", None, None, None)
    return jax.shard_map(
        per_device, mesh=fine, in_specs=in_specs, out_specs=out_specs, check_vma=False
    )
```
